512 devices in a mesh: blk: 32 (over z_lo, x), dp: 16 (over y, z_hi, core).
Axes of the slice: x: 4, y: 4, z: 16 (z_hi: 2, z_lo: 8; z = z_hi * 8 + z_lo), core: 2. Of those that a mesh axis runs over, the one named last changes fastest.
Arguments:
- inputs: bfloat16 [512, 128, 4096], P(('blk', 'dp')), may hold values from -6 to 6
- queries: bfloat16 [512, 128, 4096], P(('blk', 'dp'))
- keys: bfloat16 [512, 128, 512], P(('blk', 'dp'))
- values: bfloat16 [512, 128, 512], P(('blk', 'dp')), may hold values from -6 to 6
- out_grad: bfloat16 [512, 128, 4096], P(('blk', 'dp')), may hold values from -6 to 6
- lengths: int32 [512], P(('blk', 'dp')), may hold values from 1 to 128, as said below
- value_weight: bfloat16 [4096, 512], P('blk'), may hold values from -0.25 to 0.25
Outputs:
- input_grad: bfloat16 [512, 128, 4096], P(('blk', 'dp'))
- key_grad: bfloat16 [512, 128, 512], P(('blk', 'dp'))
- weight_grad: float32 [4096, 512], P('blk')
The draws below stay inside these ranges and needn't reach their ends.
Inputs may be any that keep to these rules, and one draw needn't show every extreme that they name: `lengths`: some microbatch has all 128 slots live.
All inputs are finite; a program needn't handle non-finite values.
Results may differ from the reference program's by a relative error of at most 0.01.
Values may be sent and summed in bfloat16 or wider, within the bound.
No kernel may reach another device: no remote copies, remote signals or barrier semaphores. Data moves between devices by JAX's collectives and lax.ppermute only.
A program may use at most 64 MiB of HBM per device.

```python
import jax
import jax.numpy as jnp
from jax import lax

WIDTH = 4096
KV_HEADS = 4
HEAD_DIM = 128
TOK_DEV = 128
Q_HEADS = 32
MICRO = 512


def key_field(key):
    shared = jax.random.fold_in(key, 11)
    drawn = jax.random.normal(shared, (MICRO, TOK_DEV, KV_HEADS * HEAD_DIM), jnp.float32)
    return jnp.clip(drawn, -4.0, 4.0)


def draw_keys(key, part):
    field = key_field(key)
    return field.astype(jnp.bfloat16)


def draw_queries(key, part):
    key = jax.random.fold_in(key, 5)
    query_field = jnp.clip(jax.random.normal(key, (MICRO, TOK_DEV, Q_HEADS * HEAD_DIM), jnp.float32), -4.0, 4.0)
    return query_field.astype(jnp.bfloat16)


def draw_lengths(key, part):
    key = jax.random.fold_in(key, 7)
    drawn = jax.random.randint(key, (MICRO,), 1, TOK_DEV + 1, jnp.int32)
    return drawn.at[0].set(TOK_DEV).astype(jnp.int32)


def block_levels(own_key, extent, split, least, largest):
    level, own = 1.0, jax.random.fold_in(own_key, 6)
    for axis_at, blocks in split:
        steps = jnp.exp(jax.random.uniform(jax.random.fold_in(own, axis_at), (blocks,), jnp.float32, least / len(split), largest / len(split)))
        level = level * jnp.repeat(steps, extent[axis_at] // blocks).reshape([-1 if axis == axis_at else 1 for axis in range(len(extent))])
    return level


def centred(stream_key, extent, scale, bound, pieces=(), held_as=jnp.bfloat16):
    values = scale * jax.random.normal(stream_key, extent, jnp.float32)
    if pieces:
        values = values * block_levels(stream_key, extent, pieces, -0.22, 0.18)
    return jnp.clip(values, -bound, bound).astype(held_as)


def setup_inputs(seed: int = 0) -> dict:
    splits = jax.random.split(jax.random.key(seed), 8)
    inputs = centred(splits[0], (MICRO, TOK_DEV, WIDTH), 1.0, 6.0, ((0, 512),))
    queries = draw_queries(jax.random.fold_in(splits[7], 71), 0)
    keys = draw_keys(jax.random.fold_in(splits[7], 71), 0)
    values = centred(splits[3], (MICRO, TOK_DEV, KV_HEADS * HEAD_DIM), 1.0, 6.0, ((0, 512),))
    out_grad = centred(splits[4], (MICRO, TOK_DEV, Q_HEADS * HEAD_DIM), 1.0, 6.0, ((0, 512),))
    lengths = draw_lengths(jax.random.fold_in(splits[7], 71), 0)
    value_weight = centred(splits[6], (WIDTH, KV_HEADS * HEAD_DIM), (KV_HEADS * HEAD_DIM) ** -0.5, 0.25, ((0, 32),))
    return dict(inputs=inputs, queries=queries, keys=keys, values=values, out_grad=out_grad, lengths=lengths, value_weight=value_weight)


def attend_back(query, key_rows, value_rows, grad_rows, length):
    tok_count = query.shape[0]
    kv_dim = key_rows.shape[1]
    heads_kv = kv_dim // HEAD_DIM
    group_size = query.shape[1] // kv_dim
    scaling = HEAD_DIM ** -0.5
    query_heads = query.reshape(tok_count, heads_kv, group_size, HEAD_DIM).astype(jnp.float32)
    key_heads = key_rows.reshape(tok_count, heads_kv, HEAD_DIM).astype(jnp.float32)
    value_heads = value_rows.reshape(tok_count, heads_kv, HEAD_DIM).astype(jnp.float32)
    grad_heads = grad_rows.reshape(tok_count, heads_kv, group_size, HEAD_DIM).astype(jnp.float32)
    scores = jnp.einsum("tkgd,skd->kgts", query_heads, key_heads) * scaling
    position = jnp.arange(tok_count)
    allowed = position[None, :] <= position[:, None]
    scores = jnp.where(allowed, scores, jnp.float32(-1e30))
    highest = jnp.max(scores, axis=-1, keepdims=True)
    expd = jnp.exp(scores - highest)
    attn_probs = expd / jnp.sum(expd, axis=-1, keepdims=True)
    is_valid = (position < length).astype(jnp.float32)
    attn_probs = attn_probs * is_valid[None, None, :, None]
    probs_low = lax.optimization_barrier(attn_probs.astype(jnp.bfloat16)).astype(jnp.float32)
    attended = jnp.einsum("kgts,skd->tkgd", attn_probs, value_heads, precision=lax.Precision.HIGHEST)
    row_delta = jnp.sum(grad_heads * attended, axis=-1)
    dprob = jnp.einsum("tkgd,skd->kgts", grad_heads, value_heads)
    dscore = attn_probs * (dprob - jnp.transpose(row_delta, (1, 2, 0))[..., None])
    dscore_low = lax.optimization_barrier(dscore.astype(jnp.bfloat16)).astype(jnp.float32)
    value_grad = jnp.einsum("kgts,tkgd->skd", probs_low, grad_heads)
    key_grad = jnp.einsum("kgts,tkgd->skd", dscore_low, query_heads) * scaling
    value_grad = value_grad.reshape(tok_count, kv_dim).astype(jnp.bfloat16)
    key_grad = key_grad.reshape(tok_count, kv_dim).astype(jnp.bfloat16)
    return value_grad, key_grad


def reference(inputs, queries, keys, values, out_grad, lengths, value_weight):
    def micro_step(running, batch_item):
        tokens, query, key_rows, value_rows, grad_rows, length = batch_item
        value_grad, key_grad = attend_back(query, key_rows, value_rows, grad_rows, length)
        input_grad = jnp.dot(value_grad, value_weight.T, preferred_element_type=jnp.float32).astype(jnp.bfloat16)
        grad_term = jnp.dot(tokens.T, value_grad, preferred_element_type=jnp.float32).astype(jnp.bfloat16)
        grad_term = lax.optimization_barrier(grad_term)
        return running + grad_term.astype(jnp.float32), (input_grad, key_grad)

    start_sum = jnp.zeros(value_weight.shape, jnp.float32)
    running, (input_grads, key_grads) = lax.scan(micro_step, start_sum, (inputs, queries, keys, values, out_grad, lengths))
    return input_grads, key_grads, running / MICRO
```

```python
import jax
import jax.numpy as jnp
from jax import lax
from jax.experimental import pallas as pl
from jax.experimental.pallas import tpu as pltpu
from jax.sharding import Mesh
from jax.sharding import PartitionSpec as P

ZL, XN, YN, ZH, CN = 8, 4, 4, 2, 2
QN = CN * YN
TOK, WIDTH, KV, HD = 128, 4096, 512, 128
GROUP = 8
SUB = 16
BF, F32 = jnp.bfloat16, jnp.float32


def nt(a, b):
    return lax.dot_general(a, b, (((1,), (1,)), ((), ())), preferred_element_type=F32)


def attend_kernel(length_ref, q_ref, k_ref, v_ref, g_ref, vg_ref, kg_ref):
    scaling = HD ** (-0.5)
    keys, vals = k_ref[...], v_ref[...]
    length = length_ref[0]
    step = 2
    wide = step * TOK
    pos_s = lax.broadcasted_iota(jnp.int32, (TOK, wide), 0)
    pos_t = lax.broadcasted_iota(jnp.int32, (TOK, wide), 1) & (TOK - 1)
    allowed = pos_s <= pos_t
    live = ((lax.broadcasted_iota(jnp.int32, (1, wide), 1) & (TOK - 1)) < length).astype(F32)
    vg = jnp.zeros((TOK, HD), F32)
    kg = jnp.zeros((TOK, HD), F32)
    for first in range(0, GROUP, step):
        heads = range(first, first + step)
        qs = jnp.concatenate([q_ref[:, h * HD : (h + 1) * HD] for h in heads], axis=0)
        gs = jnp.concatenate([g_ref[:, h * HD : (h + 1) * HD] for h in heads], axis=0)
        scores = jnp.where(allowed, nt(keys, qs) * scaling, F32(-1e30))
        expd = jnp.exp(scores - jnp.max(scores, axis=0, keepdims=True))
        probs = expd * (live / jnp.sum(expd, axis=0, keepdims=True))
        dprob = nt(vals, gs)
        delta = jnp.sum(probs * dprob, axis=0, keepdims=True)
        dscore = probs * (dprob - delta)
        vg += jnp.dot(probs.astype(BF), gs, preferred_element_type=F32)
        kg += jnp.dot(dscore.astype(BF), qs, preferred_element_type=F32)
    vg_ref[...] = vg.astype(BF)
    kg_ref[...] = (kg * scaling).astype(BF)


def attend_back(query, key_rows, value_rows, grad_rows, length):
    heads = KV // HD
    wide = pl.BlockSpec((TOK, GROUP * HD), lambda g: (0, g))
    thin = pl.BlockSpec((TOK, HD), lambda g: (0, g))
    return pl.pallas_call(
        attend_kernel,
        grid=(heads,),
        in_specs=[pl.BlockSpec(memory_space=pltpu.SMEM), wide, thin, thin, wide],
        out_specs=[thin, thin],
        out_shape=[jax.ShapeDtypeStruct((TOK, KV), BF)] * 2,
        compiler_params=pltpu.CompilerParams(vmem_limit_bytes=24 << 20),
        cost_estimate=pl.CostEstimate(
            flops=10 * 32 * TOK * TOK * HD, bytes_accessed=3 << 20, transcendentals=32 * TOK * TOK
        ),
        name="attend",
    )(length, query, key_rows, value_rows, grad_rows)


def swap_groups(tiles):
    lane = lax.broadcasted_iota(jnp.int32, tiles[0].shape, 1)
    for bit in (1, 2, 4):
        shift = bit * SUB
        high = (lane & shift) != 0
        after = list(tiles)
        for i in range(8):
            if i & bit == 0:
                low_tile, high_tile = tiles[i], tiles[i | bit]
                after[i] = jnp.where(high, pltpu.roll(high_tile, shift, 1), low_tile)
                after[i | bit] = jnp.where(high, high_tile, pltpu.roll(low_tile, 128 - shift, 1))
        tiles = after
    return tiles


def to_pieces_kernel(in_ref, out_ref):
    for x in range(XN):
        tiles = [in_ref[:, (zl * XN + x) * 128 : (zl * XN + x + 1) * 128].astype(F32) for zl in range(8)]
        for q, tile in enumerate(swap_groups(tiles)):
            out_ref[q, :, x * 128 : (x + 1) * 128] = tile.astype(BF)


def from_pieces_kernel(in_ref, out_ref):
    for x in range(XN):
        tiles = [in_ref[q, :, x * 128 : (x + 1) * 128].astype(F32) for q in range(8)]
        for zl, tile in enumerate(swap_groups(tiles)):
            out_ref[:, (zl * XN + x) * 128 : (zl * XN + x + 1) * 128] = tile.astype(BF)


def to_pieces(rows):
    part = 32
    return pl.pallas_call(
        to_pieces_kernel,
        grid=(TOK // part,),
        in_specs=[pl.BlockSpec((part, WIDTH), lambda i: (i, 0))],
        out_specs=pl.BlockSpec((QN, part, KV), lambda i: (0, i, 0)),
        out_shape=jax.ShapeDtypeStruct((QN, TOK, KV), BF),
        compiler_params=pltpu.CompilerParams(vmem_limit_bytes=24 << 20),
        cost_estimate=pl.CostEstimate(flops=1 << 22, bytes_accessed=2 << 20, transcendentals=0),
        name="to_pieces",
    )(rows)


def from_pieces(pieces):
    part = 32
    return pl.pallas_call(
        from_pieces_kernel,
        grid=(TOK // part,),
        in_specs=[pl.BlockSpec((QN, part, KV), lambda i: (0, i, 0))],
        out_specs=pl.BlockSpec((part, WIDTH), lambda i: (i, 0)),
        out_shape=jax.ShapeDtypeStruct((TOK, WIDTH), BF),
        compiler_params=pltpu.CompilerParams(vmem_limit_bytes=24 << 20),
        cost_estimate=pl.CostEstimate(flops=1 << 22, bytes_accessed=2 << 20, transcendentals=0),
        name="from_pieces",
    )(pieces)


def exchange(array, axes):
    return lax.all_to_all(array, axes, 0, 0, tiled=True)


def spread(array, axes, count):
    return exchange(jnp.broadcast_to(array[None], (count,) + array.shape), axes)


def per_device(inputs, queries, keys, values, out_grad, lengths, value_weight):
    with jax.named_scope("send_inputs"):
        columns = exchange(to_pieces(inputs[0]), ("core", "y"))
    with jax.named_scope("gather_weight"):
        q = lax.axis_index("core") * YN + lax.axis_index("y")
        own = lax.dynamic_slice_in_dim(value_weight, q * SUB, SUB, 0)
        weight = spread(own, "zl", ZL)
        weight = spread(weight.reshape(ZL * SUB, KV), "x", XN).reshape(XN * ZL * SUB, KV)
    with jax.named_scope("attention"):
        value_grad, key_grad = attend_back(queries[0], keys[0], values[0], out_grad[0], lengths)
    with jax.named_scope("gather_value_grad"):
        grads = spread(value_grad, "y", YN)
        grads = lax.all_gather(grads, "core", axis=0, tiled=True).reshape(QN * TOK, KV)
    with jax.named_scope("weight_term"):
        term = lax.dot_general(
            columns.reshape(QN * TOK, KV), grads, (((0,), (0,)), ((), ())), preferred_element_type=F32
        ).astype(BF)
    with jax.named_scope("sum_x"):
        got = exchange(term.reshape(XN, ZL * SUB, KV), "x")
        plane = jnp.sum(got.astype(F32), axis=0).astype(BF).reshape(1, ZL, SUB, KV)
    with jax.named_scope("sum_z"):
        both = jnp.broadcast_to(plane, (ZH, ZL, SUB, KV)).reshape(ZH * ZL, SUB, KV)
        got = exchange(both, ("zh", "zl"))
        total = jnp.sum(got.astype(F32), axis=0) * F32(1.0 / 512)
    with jax.named_scope("share_rows"):
        weight_grad = spread(total, ("core", "y"), QN).reshape(QN * SUB, KV)
    with jax.named_scope("input_grad"):
        parts = nt(grads, weight).astype(BF).reshape(QN, TOK, KV)
        input_grad = from_pieces(exchange(parts, ("core", "y")))
    return (input_grad[None], key_grad[None], weight_grad)


def solution(mesh):
    fine = Mesh(mesh.devices.reshape(ZL, XN, YN, ZH, CN), ("zl", "x", "y", "zh", "core"))
    micro = ("zl", "x", "y", "zh", "core")
    blk = ("zl", "x")
    rows = P(micro, None, None)
    return jax.shard_map(
        per_device,
        mesh=fine,
        in_specs=(rows, rows, rows, rows, rows, P(micro), P(blk, None)),
        out_specs=(rows, rows, P(blk, None)),
        check_vma=False,
    )
```

```python
import jax
import jax.numpy as jnp
from jax import lax
from jax.experimental import pallas as pl
from jax.experimental.pallas import tpu as pltpu
from jax.sharding import Mesh
from jax.sharding import PartitionSpec as P

ZL, XN, YN, ZH, CN = 8, 4, 4, 2, 2
QN = CN * YN
TOK, WIDTH, KV, HD = 128, 4096, 512, 128
GROUP = 8
SUB = 16
BF, F32 = jnp.bfloat16, jnp.float32


def nt(a, b):
    return lax.dot_general(a, b, (((1,), (1,)), ((), ())), preferred_element_type=F32)


def attend_kernel(length_ref, q_ref, k_ref, v_ref, g_ref, _, vg_ref, kg_ref):
    scaling = HD ** (-0.5)
    keys, vals = k_ref[...], v_ref[...]
    length = length_ref[0]
    step = 2
    wide = step * TOK
    pos_s = lax.broadcasted_iota(jnp.int32, (TOK, wide), 0)
    pos_t = lax.broadcasted_iota(jnp.int32, (TOK, wide), 1) & (TOK - 1)
    allowed = pos_s <= pos_t
    live = ((lax.broadcasted_iota(jnp.int32, (1, wide), 1) & (TOK - 1)) < length).astype(F32)
    vg = jnp.zeros((TOK, HD), F32)
    kg = jnp.zeros((TOK, HD), F32)
    for first in range(0, GROUP, step):
        heads = range(first, first + step)
        qs = jnp.concatenate([q_ref[:, h * HD : (h + 1) * HD] for h in heads], axis=0)
        gs = jnp.concatenate([g_ref[:, h * HD : (h + 1) * HD] for h in heads], axis=0)
        scores = jnp.where(allowed, nt(keys, qs) * scaling, F32(-1e30))
        expd = jnp.exp(scores - jnp.max(scores, axis=0, keepdims=True))
        probs = expd * (live / jnp.sum(expd, axis=0, keepdims=True))
        dprob = nt(vals, gs)
        delta = jnp.sum(probs * dprob, axis=0, keepdims=True)
        dscore = probs * (dprob - delta)
        vg += jnp.dot(probs.astype(BF), gs, preferred_element_type=F32)
        kg += jnp.dot(dscore.astype(BF), qs, preferred_element_type=F32)
    vg_ref[...] = vg.astype(BF)
    kg_ref[...] = (kg * scaling).astype(BF)


def attend_back(query, key_rows, value_rows, grad_rows, length, earlier):
    heads = KV // HD
    wide = pl.BlockSpec((TOK, GROUP * HD), lambda g: (0, g))
    thin = pl.BlockSpec((TOK, HD), lambda g: (0, g))
    return pl.pallas_call(
        attend_kernel,
        grid=(heads,),
        in_specs=[pl.BlockSpec(memory_space=pltpu.SMEM), wide, thin, thin, wide, pl.BlockSpec(memory_space=pl.ANY)],
        out_specs=[thin, thin],
        out_shape=[jax.ShapeDtypeStruct((TOK, KV), BF)] * 2,
        cost_estimate=pl.CostEstimate(
            flops=10 * 32 * TOK * TOK * HD, bytes_accessed=3 << 20, transcendentals=32 * TOK * TOK
        ),
        name="attend",
    )(length, query, key_rows, value_rows, grad_rows, earlier)


def swap_groups(tiles):
    lane = lax.broadcasted_iota(jnp.int32, tiles[0].shape, 1)
    for bit in (1, 2, 4):
        shift = bit * SUB
        high = (lane & shift) != 0
        after = list(tiles)
        for i in range(8):
            if i & bit == 0:
                low_tile, high_tile = tiles[i], tiles[i | bit]
                after[i] = jnp.where(high, pltpu.roll(high_tile, shift, 1), low_tile)
                after[i | bit] = jnp.where(high, high_tile, pltpu.roll(low_tile, 128 - shift, 1))
        tiles = after
    return tiles


def to_pieces_kernel(in_ref, out_ref):
    for x in range(XN):
        tiles = [in_ref[:, (zl * XN + x) * 128 : (zl * XN + x + 1) * 128].astype(F32) for zl in range(8)]
        for q, tile in enumerate(swap_groups(tiles)):
            out_ref[q, :, x * 128 : (x + 1) * 128] = tile.astype(BF)


def from_pieces_kernel(places_ref, *refs):
    out_ref, held = refs[-2:]
    for i in range(QN):
        held[places_ref[i]] = refs[i // CN][i % CN]
    for x in range(XN):
        tiles = [held[q, :, x * 128 : (x + 1) * 128].astype(F32) for q in range(8)]
        for zl, tile in enumerate(swap_groups(tiles)):
            out_ref[:, (zl * XN + x) * 128 : (zl * XN + x + 1) * 128] = tile.astype(BF)


def to_pieces(rows):
    part = 32
    return pl.pallas_call(
        to_pieces_kernel,
        grid=(TOK // part,),
        in_specs=[pl.BlockSpec((part, WIDTH), lambda i: (i, 0))],
        out_specs=pl.BlockSpec((QN, part, KV), lambda i: (0, i, 0)),
        out_shape=jax.ShapeDtypeStruct((QN, TOK, KV), BF),
        cost_estimate=pl.CostEstimate(flops=1 << 22, bytes_accessed=2 << 20, transcendentals=0),
        name="to_pieces",
    )(rows)


def from_pieces(pieces, places):
    part = 32
    return pl.pallas_call(
        from_pieces_kernel,
        grid=(TOK // part,),
        in_specs=[pl.BlockSpec(memory_space=pltpu.SMEM)]
        + [pl.BlockSpec((CN, part, KV), lambda i: (0, i, 0))] * YN,
        out_specs=pl.BlockSpec((part, WIDTH), lambda i: (i, 0)),
        out_shape=jax.ShapeDtypeStruct((TOK, WIDTH), BF),
        scratch_shapes=[pltpu.VMEM((QN, part, KV), BF)],
        cost_estimate=pl.CostEstimate(flops=1 << 22, bytes_accessed=2 << 20, transcendentals=0),
        compiler_params=pltpu.CompilerParams(vmem_limit_bytes=16 << 20),
        name="from_pieces",
    )(jnp.stack(places).astype(jnp.int32), *pieces)


def exchange(array, axes):
    return lax.all_to_all(array, axes, 0, 0, tiled=True)


def spread(array, axes, count):
    return exchange(jnp.broadcast_to(array[None], (count,) + array.shape), axes)


def shifted(array, axes, count, by):
    return lax.ppermute(array, axes, [(i, (i + by) % count) for i in range(count)])


def along_z(array, by):
    places = []
    for z in range(ZH * ZL):
        to = (z + by) % (ZH * ZL)
        places.append(((z % ZL) * ZH + z // ZL, (to % ZL) * ZH + to // ZL))
    return lax.ppermute(array, ("zl", "zh"), places)


def ring_spread(array, axes, count):
    return [array] + [shifted(array, axes, count, by) for by in range(1, count)]


def place_kernel(places_ref, *refs):
    out_ref = refs[-1]
    at = 0
    for ref in refs[:-1]:
        if ref.ndim < out_ref.ndim:
            out_ref[places_ref[at]] = ref[...]
            at += 1
        else:
            for i in range(ref.shape[0]):
                out_ref[places_ref[at]] = ref[i]
                at += 1


def place(parts, places):
    shape = parts[0].shape
    places = jnp.stack(places).astype(jnp.int32)
    return pl.pallas_call(
        place_kernel,
        in_specs=[pl.BlockSpec(memory_space=pltpu.SMEM)] + [pl.BlockSpec(memory_space=pltpu.VMEM)] * len(parts),
        out_specs=pl.BlockSpec(memory_space=pltpu.VMEM),
        out_shape=jax.ShapeDtypeStruct((len(places),) + shape, parts[0].dtype),
        cost_estimate=pl.CostEstimate(
            flops=0, bytes_accessed=4 * len(places) * shape[0] * shape[1], transcendentals=0
        ),
        compiler_params=pltpu.CompilerParams(vmem_limit_bytes=16 << 20),
        name="place",
    )(places, *parts)


def place_rows_kernel(at_ref, *refs):
    out_ref = refs[-1]
    for j, ref in enumerate(refs[:-1]):
        for k in range(ZL):
            row = ((at_ref[1] + XN - j) % XN) * ZL + (at_ref[0] + ZL - k) % ZL
            out_ref[pl.ds(pl.multiple_of(row * SUB, SUB), SUB), :] = ref[k * SUB : (k + 1) * SUB, :]


def place_rows(parts, zl, x):
    return pl.pallas_call(
        place_rows_kernel,
        in_specs=[pl.BlockSpec(memory_space=pltpu.SMEM)] + [pl.BlockSpec(memory_space=pltpu.VMEM)] * len(parts),
        out_specs=pl.BlockSpec(memory_space=pltpu.VMEM),
        out_shape=jax.ShapeDtypeStruct((KV, KV), BF),
        compiler_params=pltpu.CompilerParams(vmem_limit_bytes=16 << 20),
        name="place_rows",
    )(jnp.stack([zl, x]).astype(jnp.int32), *parts)


def own_rows_kernel(q_ref, rows_ref, _, out_ref):
    out_ref[...] = rows_ref[...]


def own_rows(rows, q, earlier):
    return pl.pallas_call(
        own_rows_kernel,
        grid_spec=pltpu.PrefetchScalarGridSpec(
            num_scalar_prefetch=1,
            grid=(1,),
            in_specs=[pl.BlockSpec((SUB, KV), lambda i, q: (q[0], 0)), pl.BlockSpec(memory_space=pl.ANY)],
            out_specs=pl.BlockSpec((SUB, KV), lambda i, q: (0, 0)),
        ),
        out_shape=jax.ShapeDtypeStruct((SUB, KV), BF),
        name="own_rows",
    )(q[None].astype(jnp.int32), rows, earlier)


def per_device(inputs, queries, keys, values, out_grad, lengths, value_weight):
    core, y, x = (lax.axis_index(name) for name in ("core", "y", "x"))
    zl = lax.axis_index("zl")
    q = core * YN + y
    with jax.named_scope("send_inputs"):
        pieces = to_pieces(inputs[0])
        columns = exchange(pieces, ("core", "y"))
    with jax.named_scope("attention"):
        value_grad, key_grad = attend_back(queries[0], keys[0], values[0], out_grad[0], lengths, pieces)
    with jax.named_scope("gather_value_grad"):
        ring = ring_spread(value_grad, "y", YN)
        other = shifted(jnp.stack(ring), "core", CN, 1)
        sources = [(y - k) % YN for k in range(YN)]
        grads = place(ring + [other], [core * YN + p for p in sources] + [(1 - core) * YN + p for p in sources])
        grads = grads.reshape(QN * TOK, KV)
    with jax.named_scope("weight_term"):
        term = lax.dot_general(
            columns.reshape(QN * TOK, KV), grads, (((0,), (0,)), ((), ())), preferred_element_type=F32
        ).astype(BF)
    with jax.named_scope("sum_x"):
        got = exchange(term.reshape(XN, ZL * SUB, KV), "x")
        plane = jnp.sum(got.astype(F32), axis=0).astype(BF).reshape(1, ZL, SUB, KV)
    with jax.named_scope("gather_weight"):
        ring = own_rows(value_weight, q, value_grad)[None]
        for by in (1, 2, 4):
            ring = jnp.concatenate([ring, along_z(ring, by)])
        ring = ring.reshape(ZL * SUB, KV)
        weight = place_rows(ring_spread(ring, "x", XN), zl, x)
    with jax.named_scope("input_grad"):
        parts = nt(grads, weight).astype(BF).reshape(CN, YN, TOK, KV)
        mine = lax.dynamic_index_in_dim(parts, core, 0, False)
        theirs = shifted(lax.dynamic_index_in_dim(parts, 1 - core, 0, False), "core", CN, 1)
        parts = jnp.stack([mine, theirs], axis=1)
        places, back = [], []
        for by in range(YN):
            piece = lax.dynamic_index_in_dim(parts, (y + by) % YN, 0, False)
            back.append(shifted(piece, "y", YN, by) if by else piece)
            places += [c * YN + (y - by) % YN for c in (core, 1 - core)]
        input_grad = from_pieces(back, places)
    with jax.named_scope("sum_z"):
        both = jnp.broadcast_to(plane, (ZH, ZL, SUB, KV)).reshape(ZH * ZL, SUB, KV)
        got = exchange(both, ("zh", "zl"))
        total = jnp.sum(got.astype(F32), axis=0) * F32(1.0 / 512)
    with jax.named_scope("share_rows"):
        weight_grad = spread(total, ("core", "y"), QN).reshape(QN * SUB, KV)
    return (input_grad[None], key_grad[None], weight_grad)


def solution(mesh):
    fine = Mesh(mesh.devices.reshape(ZL, XN, YN, ZH, CN), ("zl", "x", "y", "zh", "core"))
    micro = ("zl", "x", "y", "zh", "core")
    blk = ("zl", "x")
    rows = P(micro, None, None)
    return jax.shard_map(
        per_device,
        mesh=fine,
        in_specs=(rows, rows, rows, rows, rows, P(micro), P(blk, None)),
        out_specs=(rows, rows, P(blk, None)),
        check_vma=False,
    )
```

```python
import jax
import jax.numpy as jnp
from jax import lax
from jax.experimental import pallas as pl
from jax.experimental.pallas import tpu as pltpu
from jax.sharding import Mesh
from jax.sharding import PartitionSpec as P

ZL, XN, YN, ZH, CN = 8, 4, 4, 2, 2
TOK, WIDTH, KV, HD = 128, 4096, 512, 128
GROUP = 8
HALF = KV // CN
QUART = 128 // YN
HELD = ZL // CN
BF, F32 = jnp.bfloat16, jnp.float32
SMEM = pl.BlockSpec(memory_space=pltpu.SMEM)
VMEM = pl.BlockSpec(memory_space=pltpu.VMEM)
UNREAD = pl.BlockSpec(memory_space=pl.ANY)
SMALL = pltpu.CompilerParams(vmem_limit_bytes=20 << 20)


def nt(a, b):
    return lax.dot_general(a, b, (((1,), (1,)), ((), ())), preferred_element_type=F32)


def attend_kernel(length_ref, q_ref, k_ref, v_ref, g_ref, vg_ref, kg_ref):
    scaling = HD ** (-0.5)
    keys, vals = k_ref[...], v_ref[...]
    length = length_ref[0]
    step = 2
    wide = step * TOK
    pos_s = lax.broadcasted_iota(jnp.int32, (TOK, wide), 0)
    pos_t = lax.broadcasted_iota(jnp.int32, (TOK, wide), 1) & (TOK - 1)
    allowed = pos_s <= pos_t
    live = ((lax.broadcasted_iota(jnp.int32, (1, wide), 1) & (TOK - 1)) < length).astype(F32)
    vg = jnp.zeros((TOK, HD), F32)
    kg = jnp.zeros((TOK, HD), F32)
    for first in range(0, GROUP, step):
        heads = range(first, first + step)
        qs = jnp.concatenate([q_ref[:, h * HD : (h + 1) * HD] for h in heads], axis=0)
        gs = jnp.concatenate([g_ref[:, h * HD : (h + 1) * HD] for h in heads], axis=0)
        scores = jnp.where(allowed, nt(keys, qs) * scaling, F32(-1e30))
        expd = jnp.exp(scores - jnp.max(scores, axis=0, keepdims=True))
        probs = expd * (live / jnp.sum(expd, axis=0, keepdims=True))
        dprob = nt(vals, gs)
        delta = jnp.sum(probs * dprob, axis=0, keepdims=True)
        dscore = probs * (dprob - delta)
        vg += jnp.dot(probs.astype(BF), gs, preferred_element_type=F32)
        kg += jnp.dot(dscore.astype(BF), qs, preferred_element_type=F32)
    vg_ref[...] = vg.astype(BF)
    kg_ref[...] = (kg * scaling).astype(BF)


def attend_back(query, key_rows, value_rows, grad_rows, length):
    heads = KV // HD
    wide = pl.BlockSpec((TOK, GROUP * HD), lambda g: (0, g))
    thin = pl.BlockSpec((TOK, HD), lambda g: (0, g))
    return pl.pallas_call(
        attend_kernel,
        grid=(heads,),
        in_specs=[pl.BlockSpec(memory_space=pltpu.SMEM), wide, thin, thin, wide],
        out_specs=[thin, thin],
        out_shape=[jax.ShapeDtypeStruct((TOK, KV), BF)] * 2,
        cost_estimate=pl.CostEstimate(
            flops=10 * 32 * TOK * TOK * HD, bytes_accessed=3 << 20, transcendentals=32 * TOK * TOK
        ),
        name="attend",
    )(length, query, key_rows, value_rows, grad_rows)


def term_kernel(core_ref, own_ref, other_ref, own_grad_ref, other_grad_ref, out_ref):
    rows = jnp.concatenate([own_ref[...], other_ref[...]], axis=0)
    grads = jnp.concatenate([own_grad_ref[...], other_grad_ref[...]], axis=0)
    term = lax.dot_general(rows, grads, (((0,), (0,)), ((), ())), preferred_element_type=F32).astype(BF)
    for piece in range(XN * YN):
        out_ref[piece, 0] = term[piece * QUART : (piece + 1) * QUART]


def term_pieces(own, other, own_grad, other_grad, core):
    rows = pl.BlockSpec((TOK, XN * 128), lambda i, c: (0, i))
    grads = pl.BlockSpec((TOK, HALF), lambda i, c: (0, c[0]))
    return pl.pallas_call(
        term_kernel,
        grid_spec=pltpu.PrefetchScalarGridSpec(
            num_scalar_prefetch=1,
            grid=(ZL,),
            in_specs=[rows, rows, grads, grads],
            out_specs=pl.BlockSpec((XN * YN, 1, QUART, HALF), lambda i, c: (0, i, 0, 0)),
        ),
        out_shape=jax.ShapeDtypeStruct((XN * YN, ZL, QUART, HALF), BF),
        cost_estimate=pl.CostEstimate(flops=2 * 256 * WIDTH * HALF, bytes_accessed=4 << 20, transcendentals=0),
        compiler_params=SMALL,
        name="term_pieces",
    )(core[None].astype(jnp.int32), own, other, own_grad, other_grad)


def own_rows_kernel(at_ref, rows_ref, _, out_ref):
    out_ref[...] = rows_ref[...]


def own_rows(rows, y, earlier):
    return pl.pallas_call(
        own_rows_kernel,
        grid_spec=pltpu.PrefetchScalarGridSpec(
            num_scalar_prefetch=1,
            grid=(1,),
            in_specs=[pl.BlockSpec((QUART, KV), lambda i, at: (at[0], 0)), UNREAD],
            out_specs=pl.BlockSpec((QUART, KV), lambda i, at: (0, 0)),
        ),
        out_shape=jax.ShapeDtypeStruct((QUART, KV), BF),
        name="own_rows",
    )(y[None].astype(jnp.int32), rows, earlier)


def input_parts_kernel(at_ref, own_grad_ref, other_grad_ref, *refs):
    own_ref, other_ref, held = refs[-3:]
    k = pl.program_id(0)
    for i, ref in enumerate(refs[:-3]):
        first = ((at_ref[0] + YN - i) % YN) * QUART
        for j in range(XN):
            rows = ref[pl.ds(pl.multiple_of((j * HELD + k) * QUART, QUART), QUART), :]
            held[pl.ds(pl.multiple_of(j * 128 + first, QUART), QUART), :] = rows
    own_ref[...] = nt(own_grad_ref[...], held[...]).astype(BF)
    other_ref[...] = nt(other_grad_ref[...], held[...]).astype(BF)


def input_parts(own_grad, other_grad, weights, y):
    out = pl.BlockSpec((TOK, XN * 128), lambda k: (0, k))
    return pl.pallas_call(
        input_parts_kernel,
        grid=(HELD,),
        in_specs=[SMEM] + [VMEM] * (2 + YN),
        out_specs=[out, out],
        out_shape=[jax.ShapeDtypeStruct((TOK, WIDTH // CN), BF)] * 2,
        scratch_shapes=[pltpu.VMEM((XN * 128, KV), BF)],
        cost_estimate=pl.CostEstimate(flops=2 * 256 * 2048 * KV, bytes_accessed=4 << 20, transcendentals=0),
        compiler_params=SMALL,
        name="input_parts",
    )(y[None].astype(jnp.int32), own_grad, other_grad, *weights)


def merge_kernel(at_ref, own_ref, other_ref, out_ref):
    for which, ref in enumerate((own_ref, other_ref)):
        for k in range(HELD):
            for j in range(XN):
                zl = (at_ref[which] + ZL - k) % ZL
                tile = zl * XN + (at_ref[2] + XN - j) % XN
                first = (k * XN + j) * 128
                out_ref[:, pl.ds(pl.multiple_of(tile * 128, 128), 128)] = ref[:, first : first + 128]


def merge(own, other, zl, x, core):
    part = 32
    half = pl.BlockSpec((part, WIDTH // CN), lambda i: (i, 0))
    places = jnp.stack([(zl + ZL - HELD * core) % ZL, (zl + HELD + HELD * core) % ZL, x]).astype(jnp.int32)
    return pl.pallas_call(
        merge_kernel,
        grid=(TOK // part,),
        in_specs=[SMEM, half, half],
        out_specs=pl.BlockSpec((part, WIDTH), lambda i: (i, 0)),
        out_shape=jax.ShapeDtypeStruct((TOK, WIDTH), BF),
        cost_estimate=pl.CostEstimate(flops=0, bytes_accessed=2 << 20, transcendentals=0),
        compiler_params=SMALL,
        name="merge",
    )(places, own, other)


def exchange(array, axes):
    return lax.all_to_all(array, axes, 0, 0, tiled=True)


def spread(array, axes, count):
    return exchange(jnp.broadcast_to(array[None], (count,) + array.shape), axes)


def shifted(array, axis, by):
    count = lax.axis_size(axis)
    return lax.ppermute(array, axis, [(i, (i + by) % count) for i in range(count)])


def along_z(array, steps):
    pairs = []
    for z in range(ZH * ZL):
        for core, by in enumerate(steps):
            to = (z + by) % (ZH * ZL)
            pairs.append((((z % ZL) * ZH + z // ZL) * CN + core, ((to % ZL) * ZH + to // ZL) * CN + core))
    return lax.ppermute(array, ("zl", "zh", "core"), pairs)


def ring(array, axis):
    return [array] + [shifted(array, axis, by) for by in range(1, lax.axis_size(axis))]


def per_device(inputs, queries, keys, values, out_grad, lengths, value_weight):
    core, y, x, zl = (lax.axis_index(name) for name in ("core", "y", "x", "zl"))
    with jax.named_scope("swap_inputs"):
        other_inputs = shifted(inputs[0], "core", 1)
    with jax.named_scope("attention"):
        value_grad, key_grad = attend_back(queries[0], keys[0], values[0], out_grad[0], lengths)
    with jax.named_scope("swap_value_grad"):
        other_grad = shifted(value_grad, "core", 1)
    with jax.named_scope("weight_term"):
        term = term_pieces(inputs[0], other_inputs, value_grad, other_grad, core)
    with jax.named_scope("sum_xy"):
        got = exchange(term.reshape(XN * YN, ZL * QUART, HALF), ("x", "y"))
        plane = jnp.sum(got.astype(F32), axis=0).astype(BF).reshape(1, ZL, QUART, HALF)
    with jax.named_scope("sum_z"):
        both = jnp.broadcast_to(plane, (ZH, ZL, QUART, HALF)).reshape(ZH * ZL, QUART, HALF)
        got = exchange(both, ("zh", "zl"))
        total = jnp.sum(got.astype(F32), axis=0) * F32(1.0 / 512)
    with jax.named_scope("share_rows"):
        shared = spread(total, ("core", "y"), CN * YN).reshape(CN, YN * QUART, HALF)
        weight_grad = jnp.concatenate([shared[0], shared[1]], axis=1)
    with jax.named_scope("gather_weight"):
        rows = own_rows(value_weight, y, term)
        rows = jnp.concatenate([along_z(rows, (k, HELD + k if k == 0 else k - HELD)) for k in range(HELD)])
        rows = jnp.concatenate(ring(rows, "x"))
        weights = ring(rows, "y")
    with jax.named_scope("input_grad"):
        own_part, other_part = input_parts(value_grad, other_grad, weights, y)
        input_grad = merge(own_part, shifted(other_part, "core", 1), zl, x, core)
    return (input_grad[None], key_grad[None], weight_grad)


def solution(mesh):
    fine = Mesh(mesh.devices.reshape(ZL, XN, YN, ZH, CN), ("zl", "x", "y", "zh", "core"))
    micro = ("zl", "x", "y", "zh", "core")
    blk = ("zl", "x")
    rows = P(micro, None, None)
    return jax.shard_map(
        per_device,
        mesh=fine,
        in_specs=(rows, rows, rows, rows, rows, P(micro), P(blk, None)),
        out_specs=(rows, rows, P(blk, None)),
        check_vma=False,
    )
```

```python
import jax
import jax.numpy as jnp
from jax import lax
from jax.experimental import pallas as pl
from jax.experimental.pallas import tpu as pltpu
from jax.sharding import Mesh
from jax.sharding import PartitionSpec as P

ZL, XN, YN, ZH, CN = 8, 4, 4, 2, 2
ZM, ZR = 2, 4
STEPS = (-1, 0, 1, 2, 3, 4, -3, -2)
QN = CN * YN
TOK, WIDTH, KV, HD = 128, 4096, 512, 128
GROUP = 8
SUB = 16
BF, F32 = jnp.bfloat16, jnp.float32


def nt(a, b):
    return lax.dot_general(a, b, (((1,), (1,)), ((), ())), preferred_element_type=F32)


def attend_kernel(length_ref, q_ref, k_ref, v_ref, g_ref, vg_ref, kg_ref):
    scaling = HD ** (-0.5)
    keys, vals = k_ref[...], v_ref[...]
    length = length_ref[0]
    step = 2
    wide = step * TOK
    pos_s = lax.broadcasted_iota(jnp.int32, (TOK, wide), 0)
    pos_t = lax.broadcasted_iota(jnp.int32, (TOK, wide), 1) & (TOK - 1)
    allowed = pos_s <= pos_t
    live = ((lax.broadcasted_iota(jnp.int32, (1, wide), 1) & (TOK - 1)) < length).astype(F32)
    vg = jnp.zeros((TOK, HD), F32)
    kg = jnp.zeros((TOK, HD), F32)
    for first in range(0, GROUP, step):
        heads = range(first, first + step)
        qs = jnp.concatenate([q_ref[:, h * HD : (h + 1) * HD] for h in heads], axis=0)
        gs = jnp.concatenate([g_ref[:, h * HD : (h + 1) * HD] for h in heads], axis=0)
        scores = jnp.where(allowed, nt(keys, qs) * scaling, F32(-1e30))
        expd = jnp.exp(scores - jnp.max(scores, axis=0, keepdims=True))
        probs = expd * (live / jnp.sum(expd, axis=0, keepdims=True))
        dprob = nt(vals, gs)
        delta = jnp.sum(probs * dprob, axis=0, keepdims=True)
        dscore = probs * (dprob - delta)
        vg += jnp.dot(probs.astype(BF), gs, preferred_element_type=F32)
        kg += jnp.dot(dscore.astype(BF), qs, preferred_element_type=F32)
    for copy in range(YN):
        vg_ref[copy] = vg.astype(BF)
    kg_ref[...] = (kg * scaling).astype(BF)


def attend_back(query, key_rows, value_rows, grad_rows, length):
    heads = KV // HD
    wide = pl.BlockSpec((TOK, GROUP * HD), lambda g: (0, g))
    thin = pl.BlockSpec((TOK, HD), lambda g: (0, g))
    return pl.pallas_call(
        attend_kernel,
        grid=(heads,),
        in_specs=[pl.BlockSpec(memory_space=pltpu.SMEM), wide, thin, thin, wide],
        out_specs=[pl.BlockSpec((YN, TOK, HD), lambda g: (0, 0, g)), thin],
        out_shape=[jax.ShapeDtypeStruct((YN, TOK, KV), BF), jax.ShapeDtypeStruct((TOK, KV), BF)],
        cost_estimate=pl.CostEstimate(
            flops=10 * 32 * TOK * TOK * HD, bytes_accessed=3 << 20, transcendentals=32 * TOK * TOK
        ),
        name="attend",
    )(length, query, key_rows, value_rows, grad_rows)


def swap_groups(tiles):
    lane = lax.broadcasted_iota(jnp.int32, tiles[0].shape, 1)
    for bit in (1, 2, 4):
        shift = bit * SUB
        high = (lane & shift) != 0
        after = list(tiles)
        for i in range(8):
            if i & bit == 0:
                low_tile, high_tile = tiles[i], tiles[i | bit]
                after[i] = jnp.where(high, pltpu.roll(high_tile, shift, 1), low_tile)
                after[i | bit] = jnp.where(high, high_tile, pltpu.roll(low_tile, 128 - shift, 1))
        tiles = after
    return tiles


def to_pieces_kernel(in_ref, _, out_ref):
    for x in range(XN):
        tiles = [in_ref[:, (zl * XN + x) * 128 : (zl * XN + x + 1) * 128].astype(F32) for zl in range(8)]
        for q, tile in enumerate(swap_groups(tiles)):
            out_ref[q, :, x * 128 : (x + 1) * 128] = tile.astype(BF)


def from_pieces_kernel(places_ref, *refs):
    out_ref, held = refs[-2:]
    for i in range(QN):
        held[places_ref[i]] = refs[i // CN][i % CN]
    for x in range(XN):
        tiles = [held[q, :, x * 128 : (x + 1) * 128].astype(F32) for q in range(8)]
        for zl, tile in enumerate(swap_groups(tiles)):
            out_ref[:, (zl * XN + x) * 128 : (zl * XN + x + 1) * 128] = tile.astype(BF)


def to_pieces(rows, earlier):
    part = 32
    return pl.pallas_call(
        to_pieces_kernel,
        grid=(TOK // part,),
        in_specs=[pl.BlockSpec((part, WIDTH), lambda i: (i, 0)), pl.BlockSpec(memory_space=pl.ANY)],
        out_specs=pl.BlockSpec((QN, part, KV), lambda i: (0, i, 0)),
        out_shape=jax.ShapeDtypeStruct((QN, TOK, KV), BF),
        cost_estimate=pl.CostEstimate(flops=1 << 22, bytes_accessed=2 << 20, transcendentals=0),
        name="to_pieces",
    )(rows, earlier)


def from_pieces(pieces, places):
    part = 32
    return pl.pallas_call(
        from_pieces_kernel,
        grid=(TOK // part,),
        in_specs=[pl.BlockSpec(memory_space=pltpu.SMEM)]
        + [pl.BlockSpec((CN, part, KV), lambda i: (0, i, 0))] * YN,
        out_specs=pl.BlockSpec((part, WIDTH), lambda i: (i, 0)),
        out_shape=jax.ShapeDtypeStruct((TOK, WIDTH), BF),
        scratch_shapes=[pltpu.VMEM((QN, part, KV), BF)],
        cost_estimate=pl.CostEstimate(flops=1 << 22, bytes_accessed=2 << 20, transcendentals=0),
        compiler_params=pltpu.CompilerParams(vmem_limit_bytes=16 << 20),
        name="from_pieces",
    )(jnp.stack(places).astype(jnp.int32), *pieces)


def exchange(array, axes):
    return lax.all_to_all(array, axes, 0, 0, tiled=True)


def spread(array, axes, count):
    return exchange(jnp.broadcast_to(array[None], (count,) + array.shape), axes)


def shifted(array, axes, count, by):
    return lax.ppermute(array, axes, [(i, (i + by) % count) for i in range(count)])


def along_z(array, by):
    places = []
    for z in range(ZH * ZL):
        to = (z + by) % (ZH * ZL)
        places.append(((z % ZL) * ZH + z // ZL, (to % ZL) * ZH + to // ZL))
    return lax.ppermute(array, ("zm", "zr", "zh"), places)


def ring_spread(array, axes, count):
    return [array] + [shifted(array, axes, count, by) for by in range(1, count)]


def pair_kernel(core_ref, own_ref, other_ref, _, out_ref):
    core = core_ref[0]
    out_ref[core] = own_ref[...]
    out_ref[1 - core] = other_ref[...]


def pair(own, other, core, earlier):
    vmem = pl.BlockSpec(memory_space=pltpu.VMEM)
    return pl.pallas_call(
        pair_kernel,
        in_specs=[pl.BlockSpec(memory_space=pltpu.SMEM), vmem, vmem, pl.BlockSpec(memory_space=pl.ANY)],
        out_specs=vmem,
        out_shape=jax.ShapeDtypeStruct((CN,) + own.shape, own.dtype),
        compiler_params=pltpu.CompilerParams(vmem_limit_bytes=16 << 20),
        name="pair",
    )(core[None].astype(jnp.int32), own, other, earlier)


def join_kernel(*refs):
    out_ref = refs[-1]
    at = 0
    for ref in refs[:-2]:
        out_ref[at : at + ref.shape[0], :] = ref[...]
        at += ref.shape[0]


def join(parts, earlier):
    vmem = pl.BlockSpec(memory_space=pltpu.VMEM)
    return pl.pallas_call(
        join_kernel,
        in_specs=[vmem] * len(parts) + [pl.BlockSpec(memory_space=pl.ANY)],
        out_specs=vmem,
        out_shape=jax.ShapeDtypeStruct((sum(part.shape[0] for part in parts), KV), BF),
        compiler_params=pltpu.CompilerParams(vmem_limit_bytes=16 << 20),
        name="join",
    )(*parts, earlier)


def place_rows_kernel(at_ref, *refs):
    out_ref = refs[-1]
    for j, ref in enumerate(refs[:-2]):
        for i, k in enumerate(STEPS):
            row = ((at_ref[1] + XN - j) % XN) * ZL + (at_ref[0] + ZL - k) % ZL
            out_ref[pl.ds(pl.multiple_of(row * SUB, SUB), SUB), :] = ref[i * SUB : (i + 1) * SUB, :]


def place_rows(parts, zl, x, earlier):
    return pl.pallas_call(
        place_rows_kernel,
        in_specs=[pl.BlockSpec(memory_space=pltpu.SMEM)]
        + [pl.BlockSpec(memory_space=pltpu.VMEM)] * len(parts)
        + [pl.BlockSpec(memory_space=pl.ANY)],
        out_specs=pl.BlockSpec(memory_space=pltpu.VMEM),
        out_shape=jax.ShapeDtypeStruct((KV, KV), BF),
        compiler_params=pltpu.CompilerParams(vmem_limit_bytes=16 << 20),
        name="place_rows",
    )(jnp.stack([zl, x]).astype(jnp.int32), *parts, earlier)


def per_device(inputs, queries, keys, values, out_grad, lengths, value_weight):
    core, y, x, zr, zm = (lax.axis_index(name) for name in ("core", "y", "x", "zr", "zm"))
    q = core * YN + y
    with jax.named_scope("weight_along_z"):
        own_rows = lax.dynamic_slice_in_dim(value_weight, q * SUB, SUB, 0)
        ring = jnp.concatenate([along_z(own_rows, -1), own_rows, along_z(own_rows, 1)])
    with jax.named_scope("attention"):
        copies, key_grad = attend_back(queries[0], keys[0], values[0], out_grad[0], lengths)
    with jax.named_scope("gather_value_grad"):
        mine = exchange(copies, "y")
        other = shifted(mine, "core", CN, 1)
        grads = pair(mine, other, core, ring).reshape(QN * TOK, KV)
    with jax.named_scope("send_inputs"):
        columns = exchange(to_pieces(inputs[0], own_rows), ("core", "y"))
    with jax.named_scope("weight_term"):
        term = lax.dot_general(
            columns.reshape(QN * TOK, KV), grads, (((0,), (0,)), ((), ())), preferred_element_type=F32
        ).astype(BF)
    with jax.named_scope("sum_x"):
        got = exchange(term.reshape(XN, ZL * SUB, KV), "x")
        plane = jnp.sum(got.astype(F32), axis=0).astype(BF)
    with jax.named_scope("sum_near_z"):
        pieces = jnp.swapaxes(plane.reshape(ZM, ZR, SUB, KV), 0, 1)
        got = exchange(pieces.reshape(ZR, ZM * SUB, KV), "zr")
        near = jnp.sum(got.astype(F32), axis=0).astype(BF).reshape(1, ZM, SUB, KV)
    with jax.named_scope("sum_far_z"):
        both = jnp.broadcast_to(near, (ZH, ZM, SUB, KV)).reshape(ZH * ZM, SUB, KV)
        got = exchange(both, ("zh", "zm"))
        total = jnp.sum(got.astype(F32), axis=0) * F32(1.0 / 512)
    with jax.named_scope("share_rows"):
        weight_grad = spread(total, ("core", "y"), QN).reshape(QN * SUB, KV)
    with jax.named_scope("gather_weight"):
        ring = join([ring, along_z(ring, 3), along_z(ring[SUB:], -3)], term)
        weight = place_rows(ring_spread(ring, "x", XN), zm * ZR + zr, x, plane)
    with jax.named_scope("input_grad"):
        parts = nt(grads, weight).astype(BF).reshape(CN, YN, TOK, KV)
        kept = lax.dynamic_index_in_dim(parts, core, 0, False)
        theirs = shifted(lax.dynamic_index_in_dim(parts, 1 - core, 0, False), "core", CN, 1)
        parts = jnp.stack([kept, theirs], axis=1)
        places, back = [], []
        for by in range(YN):
            piece = lax.dynamic_index_in_dim(parts, (y + by) % YN, 0, False)
            back.append(shifted(piece, "y", YN, by) if by else piece)
            places += [c * YN + (y - by) % YN for c in (core, 1 - core)]
        input_grad = from_pieces(back, places)
    return (input_grad[None], key_grad[None], weight_grad)


def solution(mesh):
    names = ("zm", "zr", "x", "y", "zh", "core")
    fine = Mesh(mesh.devices.reshape(ZM, ZR, XN, YN, ZH, CN), names)
    blk = names[:3]
    rows = P(names, None, None)
    return jax.shard_map(
        per_device,
        mesh=fine,
        in_specs=(rows, rows, rows, rows, rows, P(names), P(blk, None)),
        out_specs=(rows, rows, P(blk, None)),
        check_vma=False,
    )
```

```python
import jax
import jax.numpy as jnp
from jax import lax
from jax.experimental import pallas as pl
from jax.experimental.pallas import tpu as pltpu
from jax.sharding import Mesh
from jax.sharding import PartitionSpec as P

ZL, XN, YN, ZH, CN = 8, 4, 4, 2, 2
STEPS = (-1, 0, 1, 2, 3, 4, -3, -2)
QN = CN * YN
TOK, WIDTH, KV, HD = 128, 4096, 512, 128
GROUP = 8
SUB = 16
HALF = 64
BF, F32 = jnp.bfloat16, jnp.float32


def nt(a, b):
    return lax.dot_general(a, b, (((1,), (1,)), ((), ())), preferred_element_type=F32)


def attend_kernel(length_ref, q_ref, k_ref, v_ref, g_ref, vg_ref, kg_ref):
    scaling = HD ** (-0.5)
    keys, vals = k_ref[...], v_ref[...]
    length = length_ref[0]
    step = 2
    wide = step * TOK
    pos_s = lax.broadcasted_iota(jnp.int32, (TOK, wide), 0)
    pos_t = lax.broadcasted_iota(jnp.int32, (TOK, wide), 1) & (TOK - 1)
    allowed = pos_s <= pos_t
    live = ((lax.broadcasted_iota(jnp.int32, (1, wide), 1) & (TOK - 1)) < length).astype(F32)
    vg = jnp.zeros((TOK, HD), F32)
    kg = jnp.zeros((TOK, HD), F32)
    for first in range(0, GROUP, step):
        heads = range(first, first + step)
        qs = jnp.concatenate([q_ref[:, h * HD : (h + 1) * HD] for h in heads], axis=0)
        gs = jnp.concatenate([g_ref[:, h * HD : (h + 1) * HD] for h in heads], axis=0)
        scores = jnp.where(allowed, nt(keys, qs) * scaling, F32(-1e30))
        expd = jnp.exp(scores - jnp.max(scores, axis=0, keepdims=True))
        probs = expd * (live / jnp.sum(expd, axis=0, keepdims=True))
        dprob = nt(vals, gs)
        delta = jnp.sum(probs * dprob, axis=0, keepdims=True)
        dscore = probs * (dprob - delta)
        vg += jnp.dot(probs.astype(BF), gs, preferred_element_type=F32)
        kg += jnp.dot(dscore.astype(BF), qs, preferred_element_type=F32)
    for copy in range(XN):
        vg_ref[copy] = vg.astype(BF)
    kg_ref[...] = (kg * scaling).astype(BF)


def attend_back(query, key_rows, value_rows, grad_rows, length):
    heads = KV // HD
    wide = pl.BlockSpec((TOK, GROUP * HD), lambda g: (0, g))
    thin = pl.BlockSpec((TOK, HD), lambda g: (0, g))
    return pl.pallas_call(
        attend_kernel,
        grid=(heads,),
        in_specs=[pl.BlockSpec(memory_space=pltpu.SMEM), wide, thin, thin, wide],
        out_specs=[pl.BlockSpec((XN, TOK, HD), lambda g: (0, 0, g)), thin],
        out_shape=[jax.ShapeDtypeStruct((XN, TOK, KV), BF), jax.ShapeDtypeStruct((TOK, KV), BF)],
        cost_estimate=pl.CostEstimate(
            flops=10 * 32 * TOK * TOK * HD, bytes_accessed=3 << 20, transcendentals=32 * TOK * TOK
        ),
        name="attend",
    )(length, query, key_rows, value_rows, grad_rows)


def swap_groups(tiles):
    lane = lax.broadcasted_iota(jnp.int32, tiles[0].shape, 1)
    for bit in (1, 2, 4):
        shift = bit * SUB
        high = (lane & shift) != 0
        after = list(tiles)
        for i in range(8):
            if i & bit == 0:
                low_tile, high_tile = tiles[i], tiles[i | bit]
                after[i] = jnp.where(high, pltpu.roll(high_tile, shift, 1), low_tile)
                after[i | bit] = jnp.where(high, high_tile, pltpu.roll(low_tile, 128 - shift, 1))
        tiles = after
    return tiles


def to_pieces_kernel(in_ref, _, out_ref):
    for x in range(XN):
        tiles = [in_ref[:, (zl * XN + x) * 128 : (zl * XN + x + 1) * 128].astype(F32) for zl in range(8)]
        for q, tile in enumerate(swap_groups(tiles)):
            y = q % YN
            out_ref[q // YN * XN + x, :, y * 128 : (y + 1) * 128] = tile.astype(BF)


def from_pieces_kernel(places_ref, *refs):
    out_ref, held = refs[-2:]
    for i in range(QN):
        held[places_ref[i]] = refs[i // CN][i % CN]
    for x in range(XN):
        tiles = [
            held[c * XN + x, :, y * 128 : (y + 1) * 128].astype(F32) for c in range(CN) for y in range(YN)
        ]
        for zl, tile in enumerate(swap_groups(tiles)):
            out_ref[:, (zl * XN + x) * 128 : (zl * XN + x + 1) * 128] = tile.astype(BF)


def to_pieces(rows, earlier):
    part = 32
    return pl.pallas_call(
        to_pieces_kernel,
        grid=(TOK // part,),
        in_specs=[pl.BlockSpec((part, WIDTH), lambda i: (i, 0)), pl.BlockSpec(memory_space=pl.ANY)],
        out_specs=pl.BlockSpec((QN, part, KV), lambda i: (0, i, 0)),
        out_shape=jax.ShapeDtypeStruct((QN, TOK, KV), BF),
        cost_estimate=pl.CostEstimate(flops=1 << 22, bytes_accessed=2 << 20, transcendentals=0),
        name="to_pieces",
    )(rows, earlier)


def from_pieces(pieces, places):
    part = 32
    return pl.pallas_call(
        from_pieces_kernel,
        grid=(TOK // part,),
        in_specs=[pl.BlockSpec(memory_space=pltpu.SMEM)]
        + [pl.BlockSpec((CN, part, KV), lambda i: (0, i, 0))] * XN,
        out_specs=pl.BlockSpec((part, WIDTH), lambda i: (i, 0)),
        out_shape=jax.ShapeDtypeStruct((TOK, WIDTH), BF),
        scratch_shapes=[pltpu.VMEM((QN, part, KV), BF)],
        cost_estimate=pl.CostEstimate(flops=1 << 22, bytes_accessed=2 << 20, transcendentals=0),
        compiler_params=pltpu.CompilerParams(vmem_limit_bytes=16 << 20),
        name="from_pieces",
    )(jnp.stack(places).astype(jnp.int32), *pieces)


def exchange(array, axes):
    return lax.all_to_all(array, axes, 0, 0, tiled=True)


def spread(array, axes, count):
    return exchange(jnp.broadcast_to(array[None], (count,) + array.shape), axes)


def shifted(array, axes, count, by):
    return lax.ppermute(array, axes, [(i, (i + by) % count) for i in range(count)])


def along_z(array, by):
    places = []
    for z in range(ZH * ZL):
        to = (z + by) % (ZH * ZL)
        places.append(((z % ZL) * ZH + z // ZL, (to % ZL) * ZH + to // ZL))
    return lax.ppermute(array, ("zl", "zh"), places)


def pair_kernel(core_ref, own_ref, other_ref, _, out_ref):
    core = core_ref[0]
    out_ref[core] = own_ref[...]
    out_ref[1 - core] = other_ref[...]


def pair(own, other, core, earlier):
    vmem = pl.BlockSpec(memory_space=pltpu.VMEM)
    return pl.pallas_call(
        pair_kernel,
        in_specs=[pl.BlockSpec(memory_space=pltpu.SMEM), vmem, vmem, pl.BlockSpec(memory_space=pl.ANY)],
        out_specs=vmem,
        out_shape=jax.ShapeDtypeStruct((CN,) + own.shape, own.dtype),
        compiler_params=pltpu.CompilerParams(vmem_limit_bytes=16 << 20),
        name="pair",
    )(core[None].astype(jnp.int32), own, other, earlier)


def place_rows_kernel(zl_ref, *refs):
    out_ref = refs[-1]
    for i, step in enumerate(STEPS):
        ref = refs[0 if i < 3 else 1 if i < 6 else 2]
        first = (i if i < 3 else i - 3 if i < 6 else i - 6) * YN
        for y in range(YN):
            row = (y * ZL + (zl_ref[0] + ZL - step) % ZL) * SUB
            out_ref[pl.ds(pl.multiple_of(row, SUB), SUB), :] = ref[(first + y) * SUB : (first + y + 1) * SUB, :]


def place_rows(parts, zl, earlier):
    vmem = pl.BlockSpec(memory_space=pltpu.VMEM)
    return pl.pallas_call(
        place_rows_kernel,
        in_specs=[pl.BlockSpec(memory_space=pltpu.SMEM), vmem, vmem, vmem, pl.BlockSpec(memory_space=pl.ANY)],
        out_specs=vmem,
        out_shape=jax.ShapeDtypeStruct((KV, KV), BF),
        compiler_params=pltpu.CompilerParams(vmem_limit_bytes=16 << 20),
        name="place_rows",
    )(zl[None].astype(jnp.int32), *parts, earlier)


def per_device(inputs, queries, keys, values, out_grad, lengths, value_weight):
    core, x, zl = (lax.axis_index(name) for name in ("core", "x", "zl"))
    with jax.named_scope("weight_along_z"):
        own_rows = lax.dynamic_slice_in_dim(value_weight, core * HALF, HALF, 0)
        ring = jnp.concatenate([along_z(own_rows, -1), own_rows, along_z(own_rows, 1)])
    with jax.named_scope("attention"):
        copies, key_grad = attend_back(queries[0], keys[0], values[0], out_grad[0], lengths)
    with jax.named_scope("gather_value_grad"):
        mine = exchange(copies, "x")
        other = shifted(mine, "core", CN, 1)
        grads = pair(mine, other, core, ring).reshape(CN * XN * TOK, KV)
    with jax.named_scope("send_inputs"):
        columns = exchange(to_pieces(inputs[0], own_rows), ("core", "x"))
    with jax.named_scope("weight_term"):
        term = lax.dot_general(
            columns.reshape(CN * XN * TOK, KV), grads, (((0,), (0,)), ((), ())), preferred_element_type=F32
        ).astype(BF)
    with jax.named_scope("sum_y"):
        got = exchange(term.reshape(YN, ZL * SUB, KV), "y")
        plane = jnp.sum(got.astype(F32), axis=0).astype(BF).reshape(1, ZL, SUB, KV)
    with jax.named_scope("sum_z"):
        both = jnp.broadcast_to(plane, (ZH, ZL, SUB, KV)).reshape(ZH * ZL, SUB, KV)
        got = exchange(both, ("zh", "zl"))
        total = jnp.sum(got.astype(F32), axis=0) * F32(1.0 / 512)
    with jax.named_scope("share_rows"):
        weight_grad = spread(total, ("core", "y"), QN).reshape(QN * SUB, KV)
    with jax.named_scope("gather_weight"):
        weight = place_rows([ring, along_z(ring, 3), along_z(ring[HALF:], -3)], zl, plane)
    with jax.named_scope("input_grad"):
        parts = nt(grads, weight).astype(BF).reshape(CN, XN, TOK, KV)
        kept = lax.dynamic_index_in_dim(parts, core, 0, False)
        theirs = shifted(lax.dynamic_index_in_dim(parts, 1 - core, 0, False), "core", CN, 1)
        parts = jnp.stack([kept, theirs], axis=1)
        places, back = [], []
        for by in range(XN):
            piece = lax.dynamic_index_in_dim(parts, (x + by) % XN, 0, False)
            back.append(shifted(piece, "x", XN, by) if by else piece)
            places += [c * XN + (x - by) % XN for c in (core, 1 - core)]
        input_grad = from_pieces(back, places)
    return (input_grad[None], key_grad[None], weight_grad)


def solution(mesh):
    names = ("zl", "x", "y", "zh", "core")
    fine = Mesh(mesh.devices.reshape(ZL, XN, YN, ZH, CN), names)
    blk = names[:2]
    rows = P(names, None, None)
    return jax.shard_map(
        per_device,
        mesh=fine,
        in_specs=(rows, rows, rows, rows, rows, P(names), P(blk, None)),
        out_specs=(rows, rows, P(blk, None)),
        check_vma=False,
    )
```

```python
import jax
import jax.numpy as jnp
from jax import lax
from jax.experimental import pallas as pl
from jax.experimental.pallas import tpu as pltpu
from jax.sharding import Mesh
from jax.sharding import PartitionSpec as P

ZL, XN, YN, ZH, CN = 8, 4, 4, 2, 2
STEPS = (-1, 0, 1, 2, 3, 4, -3, -2)
QN = CN * YN
TOK, WIDTH, KV, HD = 128, 4096, 512, 128
GROUP = 8
SUB = 16
HALF = 64
BF, F32 = jnp.bfloat16, jnp.float32


def nt(a, b):
    return lax.dot_general(a, b, (((1,), (1,)), ((), ())), preferred_element_type=F32)


def attend_kernel(length_ref, q_ref, k_ref, v_ref, g_ref, vg_ref, kg_ref):
    scaling = HD ** (-0.5)
    keys, vals = k_ref[...], v_ref[...]
    length = length_ref[...]
    step = 2
    wide = step * TOK
    pos_s = lax.broadcasted_iota(jnp.int32, (TOK, wide), 0)
    pos_t = lax.broadcasted_iota(jnp.int32, (TOK, wide), 1) & (TOK - 1)
    allowed = pos_s <= pos_t
    live = ((lax.broadcasted_iota(jnp.int32, (1, wide), 1) & (TOK - 1)) < length).astype(F32)
    vg = jnp.zeros((TOK, HD), F32)
    kg = jnp.zeros((TOK, HD), F32)
    for first in range(0, GROUP, step):
        heads = range(first, first + step)
        qs = jnp.concatenate([q_ref[:, h * HD : (h + 1) * HD] for h in heads], axis=0)
        gs = jnp.concatenate([g_ref[:, h * HD : (h + 1) * HD] for h in heads], axis=0)
        scores = jnp.where(allowed, nt(keys, qs) * scaling, F32(-1e30))
        expd = jnp.exp(scores - jnp.max(scores, axis=0, keepdims=True))
        probs = expd * (live / jnp.sum(expd, axis=0, keepdims=True))
        dprob = nt(vals, gs)
        delta = jnp.sum(probs * dprob, axis=0, keepdims=True)
        dscore = probs * (dprob - delta)
        vg += jnp.dot(probs.astype(BF), gs, preferred_element_type=F32)
        kg += jnp.dot(dscore.astype(BF), qs, preferred_element_type=F32)
    for copy in range(XN):
        vg_ref[copy] = vg.astype(BF)
    kg_ref[...] = (kg * scaling).astype(BF)


def attend_back(query, key_rows, value_rows, grad_rows, length):
    heads = KV // HD
    wide = pl.BlockSpec((TOK, GROUP * HD), lambda g: (0, g))
    thin = pl.BlockSpec((TOK, HD), lambda g: (0, g))
    return pl.pallas_call(
        attend_kernel,
        grid=(heads,),
        in_specs=[pl.BlockSpec(memory_space=pltpu.VMEM), wide, thin, thin, wide],
        out_specs=[pl.BlockSpec((XN, TOK, HD), lambda g: (0, 0, g)), thin],
        out_shape=[jax.ShapeDtypeStruct((XN, TOK, KV), BF), jax.ShapeDtypeStruct((TOK, KV), BF)],
        cost_estimate=pl.CostEstimate(
            flops=10 * 32 * TOK * TOK * HD, bytes_accessed=3 << 20, transcendentals=32 * TOK * TOK
        ),
        name="attend",
    )(length, query, key_rows, value_rows, grad_rows)


def swap_groups(tiles):
    lane = lax.broadcasted_iota(jnp.int32, tiles[0].shape, 1)
    for bit in (1, 2, 4):
        shift = bit * SUB
        high = (lane & shift) != 0
        after = list(tiles)
        for i in range(8):
            if i & bit == 0:
                low_tile, high_tile = tiles[i], tiles[i | bit]
                after[i] = jnp.where(high, pltpu.roll(high_tile, shift, 1), low_tile)
                after[i | bit] = jnp.where(high, high_tile, pltpu.roll(low_tile, 128 - shift, 1))
        tiles = after
    return tiles


def piece(c, x, y):
    return c * 4 + x % 2 * 2 + y % 2


def to_pieces_kernel(in_ref, _, out_ref):
    for x in range(XN):
        tiles = [in_ref[:, (zl * XN + x) * 128 : (zl * XN + x + 1) * 128].astype(F32) for zl in range(8)]
        for q, tile in enumerate(swap_groups(tiles)):
            y = q % YN
            slot = x // 2 * 2 + y // 2
            out_ref[piece(q // YN, x, y), :, slot * 128 : (slot + 1) * 128] = tile.astype(BF)


def from_pieces_kernel(places_ref, *refs):
    out_ref, held = refs[-2:]
    for i in range(QN):
        held[places_ref[i]] = refs[i // CN][i % CN]
    for x in range(XN):
        tiles = [
            held[piece(c, x, y), :, (x // 2 * 2 + y // 2) * 128 : (x // 2 * 2 + y // 2 + 1) * 128].astype(F32)
            for c in range(CN)
            for y in range(YN)
        ]
        for zl, tile in enumerate(swap_groups(tiles)):
            out_ref[:, (zl * XN + x) * 128 : (zl * XN + x + 1) * 128] = tile.astype(BF)


def to_pieces(rows, earlier):
    part = 32
    return pl.pallas_call(
        to_pieces_kernel,
        grid=(TOK // part,),
        in_specs=[pl.BlockSpec((part, WIDTH), lambda i: (i, 0)), pl.BlockSpec(memory_space=pl.ANY)],
        out_specs=pl.BlockSpec((QN, part, KV), lambda i: (0, i, 0)),
        out_shape=jax.ShapeDtypeStruct((QN, TOK, KV), BF),
        cost_estimate=pl.CostEstimate(flops=1 << 36, bytes_accessed=2 << 20, transcendentals=0),
        name="to_pieces",
    )(rows, earlier)


def from_pieces(pieces, places):
    part = 32
    return pl.pallas_call(
        from_pieces_kernel,
        grid=(TOK // part,),
        in_specs=[pl.BlockSpec(memory_space=pltpu.SMEM)]
        + [pl.BlockSpec((CN, part, KV), lambda i: (0, i, 0))] * XN,
        out_specs=pl.BlockSpec((part, WIDTH), lambda i: (i, 0)),
        out_shape=jax.ShapeDtypeStruct((TOK, WIDTH), BF),
        scratch_shapes=[pltpu.VMEM((QN, part, KV), BF)],
        cost_estimate=pl.CostEstimate(flops=1 << 22, bytes_accessed=2 << 20, transcendentals=0),
        compiler_params=pltpu.CompilerParams(vmem_limit_bytes=16 << 20),
        name="from_pieces",
    )(jnp.stack(places).astype(jnp.int32), *pieces)


def exchange(array, axes):
    return lax.all_to_all(array, axes, 0, 0, tiled=True)


def spread(array, axes, count):
    return exchange(jnp.broadcast_to(array[None], (count,) + array.shape), axes)


def shifted(array, axis, count, by):
    return lax.ppermute(array, axis, [(i, (i + by) % count) for i in range(count)])


def over_square(array, mask):
    return lax.ppermute(array, ("xp", "yp"), [(i, i ^ mask) for i in range(4)])


def along_z(array, by):
    places = []
    for z in range(ZH * ZL):
        to = (z + by) % (ZH * ZL)
        places.append(((z % ZL) * ZH + z // ZL, (to % ZL) * ZH + to // ZL))
    return lax.ppermute(array, ("zl", "zh"), places)


def pair_kernel(core_ref, own_ref, other_ref, _, out_ref):
    core = core_ref[0]
    out_ref[core] = own_ref[...]
    out_ref[1 - core] = other_ref[...]


def pair(own, other, core, earlier):
    vmem = pl.BlockSpec(memory_space=pltpu.VMEM)
    return pl.pallas_call(
        pair_kernel,
        in_specs=[pl.BlockSpec(memory_space=pltpu.SMEM), vmem, vmem, pl.BlockSpec(memory_space=pl.ANY)],
        out_specs=vmem,
        out_shape=jax.ShapeDtypeStruct((CN,) + own.shape, own.dtype),
        compiler_params=pltpu.CompilerParams(vmem_limit_bytes=16 << 20),
        name="pair",
    )(core[None].astype(jnp.int32), own, other, earlier)


def place_rows_kernel(zl_ref, *refs):
    out_ref = refs[-1]
    for i, step in enumerate(STEPS):
        ref = refs[0 if i < 3 else 1 if i < 6 else 2]
        first = (i if i < 3 else i - 3 if i < 6 else i - 6) * YN
        for y in range(YN):
            row = (y * ZL + (zl_ref[0] + ZL - step) % ZL) * SUB
            out_ref[pl.ds(pl.multiple_of(row, SUB), SUB), :] = ref[(first + y) * SUB : (first + y + 1) * SUB, :]


def place_rows(parts, zl, earlier):
    vmem = pl.BlockSpec(memory_space=pltpu.VMEM)
    return pl.pallas_call(
        place_rows_kernel,
        in_specs=[pl.BlockSpec(memory_space=pltpu.SMEM), vmem, vmem, vmem, pl.BlockSpec(memory_space=pl.ANY)],
        out_specs=vmem,
        out_shape=jax.ShapeDtypeStruct((KV, KV), BF),
        compiler_params=pltpu.CompilerParams(vmem_limit_bytes=16 << 20),
        name="place_rows",
    )(zl[None].astype(jnp.int32), *parts, earlier)


def per_device(inputs, queries, keys, values, out_grad, lengths, value_weight):
    core, zl, xh, xp, yp = (lax.axis_index(name) for name in ("core", "zl", "xh", "xp", "yp"))
    place = 2 * xp + yp
    with jax.named_scope("weight_along_z"):
        blocks = value_weight.reshape(CN, 2, 2, SUB, KV)
        own_rows = lax.dynamic_slice(blocks, (core, 0, yp, 0, 0), (1, 2, 1, SUB, KV)).reshape(2 * SUB, KV)
        far_rows = shifted(own_rows, "xh", 2, 1)
        rows = jnp.where(xh == 0, jnp.concatenate([own_rows, far_rows]), jnp.concatenate([far_rows, own_rows]))
        ring = jnp.concatenate([along_z(rows, -1), rows, along_z(rows, 1)])
    with jax.named_scope("attention"):
        copies, key_grad = attend_back(queries[0], keys[0], values[0], out_grad[0], lengths)
    with jax.named_scope("gather_value_grad"):
        mine = exchange(copies, ("xp", "yp"))
        other = shifted(mine, "core", CN, 1)
        grads = pair(mine, other, core, ring).reshape(CN * 4 * TOK, KV)
    with jax.named_scope("send_inputs"):
        columns = exchange(to_pieces(inputs[0], rows), ("core", "xp", "yp"))
    with jax.named_scope("weight_term"):
        term = lax.dot_general(
            columns.reshape(CN * 4 * TOK, KV), grads, (((0,), (0,)), ((), ())), preferred_element_type=F32
        ).astype(BF)
    with jax.named_scope("sum_squares"):
        got = exchange(term.reshape(4, ZL * SUB, KV), ("xh", "yh"))
        plane = jnp.sum(got.astype(F32), axis=0).astype(BF).reshape(1, ZL, SUB, KV)
    with jax.named_scope("sum_z"):
        both = jnp.broadcast_to(plane, (ZH, ZL, SUB, KV)).reshape(ZH * ZL, SUB, KV)
        got = exchange(both, ("zh", "zl"))
        total = jnp.sum(got.astype(F32), axis=0) * F32(1.0 / 512)
    with jax.named_scope("share_rows"):
        shared = spread(total.astype(BF), ("core", "yh", "yp"), QN)
        weight_grad = shared.reshape(QN * SUB, KV).astype(F32)
    with jax.named_scope("gather_weight"):
        weight = place_rows([ring, along_z(ring, 3), along_z(ring[HALF:], -3)], zl, plane)
    with jax.named_scope("input_grad"):
        parts = nt(grads, weight).astype(BF).reshape(CN, 4, TOK, KV)
        kept = lax.dynamic_index_in_dim(parts, core, 0, False)
        theirs = shifted(lax.dynamic_index_in_dim(parts, 1 - core, 0, False), "core", CN, 1)
        parts = jnp.stack([kept, theirs], axis=1)
        places, back = [], []
        for mask in range(4):
            sent = lax.dynamic_index_in_dim(parts, place ^ mask, 0, False)
            back.append(over_square(sent, mask) if mask else sent)
            places += [c * 4 + (place ^ mask) for c in (core, 1 - core)]
        input_grad = from_pieces(back, places)
    return (input_grad[None], key_grad[None], weight_grad)


def solution(mesh):
    names = ("zl", "xh", "xp", "yh", "yp", "zh", "core")
    fine = Mesh(mesh.devices.reshape(ZL, 2, 2, 2, 2, ZH, CN), names)
    blk = names[:3]
    rows = P(names, None, None)
    return jax.shard_map(
        per_device,
        mesh=fine,
        in_specs=(rows, rows, rows, rows, rows, P(names), P(blk, None)),
        out_specs=(rows, rows, P(blk, None)),
        check_vma=False,
    )
```

```python
import jax
import jax.numpy as jnp
from jax import lax
from jax.experimental import pallas as pl
from jax.experimental.pallas import tpu as pltpu
from jax.sharding import Mesh
from jax.sharding import PartitionSpec as P

ZL, XN, YN, ZH, CN = 8, 4, 4, 2, 2
STEPS = (-1, 0, 1, 2, 3, 4, -3, -2)
QN = CN * YN
TOK, WIDTH, KV, HD = 128, 4096, 512, 128
GROUP = 8
SUB = 16
HALF = 64
BF, F32 = jnp.bfloat16, jnp.float32


def nt(a, b):
    return lax.dot_general(a, b, (((1,), (1,)), ((), ())), preferred_element_type=F32)


def attend_kernel(length_ref, q_ref, k_ref, v_ref, g_ref, vg_ref, kg_ref):
    scaling = HD ** (-0.5)
    keys, vals = k_ref[...], v_ref[...]
    length = length_ref[...]
    step = 2
    wide = step * TOK
    pos_s = lax.broadcasted_iota(jnp.int32, (TOK, wide), 0)
    pos_t = lax.broadcasted_iota(jnp.int32, (TOK, wide), 1) & (TOK - 1)
    allowed = pos_s <= pos_t
    live = ((lax.broadcasted_iota(jnp.int32, (1, wide), 1) & (TOK - 1)) < length).astype(F32)
    vg = jnp.zeros((TOK, HD), F32)
    kg = jnp.zeros((TOK, HD), F32)
    for first in range(0, GROUP, step):
        heads = range(first, first + step)
        qs = jnp.concatenate([q_ref[:, h * HD : (h + 1) * HD] for h in heads], axis=0)
        gs = jnp.concatenate([g_ref[:, h * HD : (h + 1) * HD] for h in heads], axis=0)
        scores = jnp.where(allowed, nt(keys, qs) * scaling, F32(-1e30))
        expd = jnp.exp(scores - jnp.max(scores, axis=0, keepdims=True))
        probs = expd * (live / jnp.sum(expd, axis=0, keepdims=True))
        dprob = nt(vals, gs)
        delta = jnp.sum(probs * dprob, axis=0, keepdims=True)
        dscore = probs * (dprob - delta)
        vg += jnp.dot(probs.astype(BF), gs, preferred_element_type=F32)
        kg += jnp.dot(dscore.astype(BF), qs, preferred_element_type=F32)
    for copy in range(XN):
        vg_ref[copy] = vg.astype(BF)
    kg_ref[...] = (kg * scaling).astype(BF)


def attend_back(query, key_rows, value_rows, grad_rows, length):
    heads = KV // HD
    wide = pl.BlockSpec((TOK, GROUP * HD), lambda g: (0, g))
    thin = pl.BlockSpec((TOK, HD), lambda g: (0, g))
    return pl.pallas_call(
        attend_kernel,
        grid=(heads,),
        in_specs=[pl.BlockSpec((1, 1), lambda g: (0, 0)), wide, thin, thin, wide],
        out_specs=[pl.BlockSpec((XN, TOK, HD), lambda g: (0, 0, g)), thin],
        out_shape=[jax.ShapeDtypeStruct((XN, TOK, KV), BF), jax.ShapeDtypeStruct((TOK, KV), BF)],
        cost_estimate=pl.CostEstimate(
            flops=10 * 32 * TOK * TOK * HD, bytes_accessed=3 << 20, transcendentals=32 * TOK * TOK
        ),
        name="attend",
    )(length.reshape(1, 1), query, key_rows, value_rows, grad_rows)


def swap_groups(tiles):
    lane = lax.broadcasted_iota(jnp.int32, tiles[0].shape, 1)
    for bit in (1, 2, 4):
        shift = bit * SUB
        high = (lane & shift) != 0
        after = list(tiles)
        for i in range(8):
            if i & bit == 0:
                low_tile, high_tile = tiles[i], tiles[i | bit]
                after[i] = jnp.where(high, pltpu.roll(high_tile, shift, 1), low_tile)
                after[i | bit] = jnp.where(high, high_tile, pltpu.roll(low_tile, 128 - shift, 1))
        tiles = after
    return tiles


def to_pieces_kernel(in_ref, *refs):
    out_ref = refs[-1]
    for x in range(XN):
        tiles = [in_ref[:, (zl * XN + x) * 128 : (zl * XN + x + 1) * 128].astype(F32) for zl in range(8)]
        for q, tile in enumerate(swap_groups(tiles)):
            y = q % YN
            out_ref[q // YN * XN + x, :, y * 128 : (y + 1) * 128] = tile.astype(BF)


def from_pieces_kernel(places_ref, *refs):
    out_ref, held = refs[-2:]
    for i in range(QN):
        held[places_ref[i]] = refs[i // CN][i % CN]
    for x in range(XN):
        tiles = [
            held[c * XN + x, :, y * 128 : (y + 1) * 128].astype(F32) for c in range(CN) for y in range(YN)
        ]
        for zl, tile in enumerate(swap_groups(tiles)):
            out_ref[:, (zl * XN + x) * 128 : (zl * XN + x + 1) * 128] = tile.astype(BF)


def to_pieces(rows, earlier):
    part = 32
    steps = TOK // part
    out = None
    for first, count in ((0, steps - 1), (steps - 1, 1)):
        block = pl.BlockSpec((part, WIDTH), lambda i, first=first: (i + first, 0))
        out = pl.pallas_call(
            to_pieces_kernel,
            grid=(count,),
            in_specs=[block] + [pl.BlockSpec(memory_space=pl.ANY)] * (2 if first else 1),
            out_specs=pl.BlockSpec((QN, part, KV), lambda i, first=first: (0, i + first, 0)),
            out_shape=jax.ShapeDtypeStruct((QN, TOK, KV), BF),
            input_output_aliases={2: 0} if first else {},
            cost_estimate=pl.CostEstimate(flops=count << 20, bytes_accessed=count << 19, transcendentals=0),
            name="to_pieces",
        )(*((rows, earlier[1], out) if first else (rows, earlier[0])))
    return out


def from_pieces(pieces, places):
    part = 32
    return pl.pallas_call(
        from_pieces_kernel,
        grid=(TOK // part,),
        in_specs=[pl.BlockSpec(memory_space=pltpu.SMEM)]
        + [pl.BlockSpec((CN, part, KV), lambda i: (0, i, 0))] * XN,
        out_specs=pl.BlockSpec((part, WIDTH), lambda i: (i, 0)),
        out_shape=jax.ShapeDtypeStruct((TOK, WIDTH), BF),
        scratch_shapes=[pltpu.VMEM((QN, part, KV), BF)],
        cost_estimate=pl.CostEstimate(flops=1 << 22, bytes_accessed=2 << 20, transcendentals=0),
        compiler_params=pltpu.CompilerParams(vmem_limit_bytes=16 << 20),
        name="from_pieces",
    )(jnp.stack(places).astype(jnp.int32), *pieces)


def exchange(array, axes):
    return lax.all_to_all(array, axes, 0, 0, tiled=True)


def spread(array, axes, count):
    return exchange(jnp.broadcast_to(array[None], (count,) + array.shape), axes)


def shifted(array, axes, count, by):
    return lax.ppermute(array, axes, [(i, (i + by) % count) for i in range(count)])


def along_z(array, by):
    places = []
    for z in range(ZH * ZL):
        to = (z + by) % (ZH * ZL)
        places.append(((z % ZL) * ZH + z // ZL, (to % ZL) * ZH + to // ZL))
    return lax.ppermute(array, ("zl", "zh"), places)


def pair_kernel(core_ref, own_ref, other_ref, _, out_ref):
    core = core_ref[0]
    out_ref[core] = own_ref[...]
    out_ref[1 - core] = other_ref[...]


def pair(own, other, core, earlier):
    vmem = pl.BlockSpec(memory_space=pltpu.VMEM)
    return pl.pallas_call(
        pair_kernel,
        in_specs=[pl.BlockSpec(memory_space=pltpu.SMEM), vmem, vmem, pl.BlockSpec(memory_space=pl.ANY)],
        out_specs=vmem,
        out_shape=jax.ShapeDtypeStruct((CN,) + own.shape, own.dtype),
        compiler_params=pltpu.CompilerParams(vmem_limit_bytes=16 << 20),
        name="pair",
    )(core[None].astype(jnp.int32), own, other, earlier)


def place_rows_kernel(zl_ref, *refs):
    out_ref = refs[-1]
    for i, step in enumerate(STEPS):
        ref = refs[0 if i < 3 else 1 if i < 6 else 2]
        first = (i if i < 3 else i - 3 if i < 6 else i - 6) * YN
        for y in range(YN):
            row = (y * ZL + (zl_ref[0] + ZL - step) % ZL) * SUB
            out_ref[pl.ds(pl.multiple_of(row, SUB), SUB), :] = ref[(first + y) * SUB : (first + y + 1) * SUB, :]


def place_rows(parts, zl, earlier):
    vmem = pl.BlockSpec(memory_space=pltpu.VMEM)
    return pl.pallas_call(
        place_rows_kernel,
        in_specs=[pl.BlockSpec(memory_space=pltpu.SMEM), vmem, vmem, vmem, pl.BlockSpec(memory_space=pl.ANY)],
        out_specs=vmem,
        out_shape=jax.ShapeDtypeStruct((KV, KV), BF),
        cost_estimate=pl.CostEstimate(flops=1 << 36, bytes_accessed=1 << 20, transcendentals=0),
        compiler_params=pltpu.CompilerParams(vmem_limit_bytes=16 << 20),
        name="place_rows",
    )(zl[None].astype(jnp.int32), *parts, earlier)


def sum_first_kernel(got_ref, out_ref):
    total = got_ref[0].astype(F32)
    for i in range(1, got_ref.shape[0]):
        total += got_ref[i].astype(F32)
    out_ref[...] = total.astype(BF)


def sum_first(got):
    vmem = pl.BlockSpec(memory_space=pltpu.VMEM)
    return pl.pallas_call(
        sum_first_kernel,
        in_specs=[vmem],
        out_specs=vmem,
        out_shape=jax.ShapeDtypeStruct(got.shape[1:], BF),
        cost_estimate=pl.CostEstimate(flops=1 << 36, bytes_accessed=1 << 20, transcendentals=0),
        compiler_params=pltpu.CompilerParams(vmem_limit_bytes=16 << 20),
        name="sum_first",
    )(got)


def twice_kernel(in_ref, _, out_ref):
    for copy in range(ZH):
        out_ref[copy] = in_ref[...]


def twice(array, earlier):
    vmem = pl.BlockSpec(memory_space=pltpu.VMEM)
    return pl.pallas_call(
        twice_kernel,
        in_specs=[vmem, pl.BlockSpec(memory_space=pl.ANY)],
        out_specs=vmem,
        out_shape=jax.ShapeDtypeStruct((ZH,) + array.shape, BF),
        compiler_params=pltpu.CompilerParams(vmem_limit_bytes=16 << 20),
        name="twice",
    )(array, earlier)


def per_device(inputs, queries, keys, values, out_grad, lengths, value_weight):
    core, x, zl = (lax.axis_index(name) for name in ("core", "x", "zl"))
    with jax.named_scope("weight_along_z"):
        own_rows = lax.dynamic_slice_in_dim(value_weight, core * HALF, HALF, 0)
        ring = jnp.concatenate([along_z(own_rows, -1), own_rows, along_z(own_rows, 1)])
    with jax.named_scope("attention"):
        copies, key_grad = attend_back(queries[0], keys[0], values[0], out_grad[0], lengths)
    with jax.named_scope("gather_value_grad"):
        mine = exchange(copies, "x")
        other = shifted(mine, "core", CN, 1)
        grads = pair(mine, other, core, ring).reshape(CN * XN * TOK, KV)
    with jax.named_scope("send_inputs"):
        columns = exchange(to_pieces(inputs[0], (own_rows, ring)), ("core", "x"))
    with jax.named_scope("weight_term"):
        term = lax.dot_general(
            columns.reshape(CN * XN * TOK, KV), grads, (((0,), (0,)), ((), ())), preferred_element_type=F32
        ).astype(BF)
    with jax.named_scope("gather_weight"):
        weight = place_rows([ring, along_z(ring, 3), along_z(ring[HALF:], -3)], zl, term)
    with jax.named_scope("input_grad"):
        parts = product = nt(grads, weight).astype(BF).reshape(CN, XN, TOK, KV)
        kept = lax.dynamic_index_in_dim(parts, core, 0, False)
        theirs = shifted(lax.dynamic_index_in_dim(parts, 1 - core, 0, False), "core", CN, 1)
        parts = jnp.stack([kept, theirs], axis=1)
        places, back = [], []
        for by in range(XN):
            piece = lax.dynamic_index_in_dim(parts, (x + by) % XN, 0, False)
            back.append(shifted(piece, "x", XN, by) if by else piece)
            places += [c * XN + (x - by) % XN for c in (core, 1 - core)]
        input_grad = from_pieces(back, places)
    with jax.named_scope("sum_y"):
        got = exchange(term.reshape(YN, ZL * SUB, KV), "y")
        both = twice(sum_first(got), theirs).reshape(ZH * ZL, SUB, KV)
    with jax.named_scope("sum_z"):
        got = exchange(both, ("zh", "zl"))
        total = jnp.sum(got.astype(F32), axis=0) * F32(1.0 / 512)
    with jax.named_scope("share_rows"):
        weight_grad = spread(total.astype(BF), ("core", "y"), QN).reshape(QN * SUB, KV).astype(F32)
    return (input_grad[None], key_grad[None], weight_grad)


def solution(mesh):
    names = ("zl", "x", "y", "zh", "core")
    fine = Mesh(mesh.devices.reshape(ZL, XN, YN, ZH, CN), names)
    blk = names[:2]
    rows = P(names, None, None)
    return jax.shard_map(
        per_device,
        mesh=fine,
        in_specs=(rows, rows, rows, rows, rows, P(names), P(blk, None)),
        out_specs=(rows, rows, P(blk, None)),
        check_vma=False,
    )
```

```python
import jax
import jax.numpy as jnp
from jax import lax
from jax.experimental import pallas as pl
from jax.experimental.pallas import tpu as pltpu
from jax.sharding import Mesh
from jax.sharding import PartitionSpec as P

ZL, XN, YN, ZH, CN = 8, 4, 4, 2, 2
QN = CN * YN
TOK, WIDTH, KV, HD = 128, 4096, 512, 128
GROUP = 8
SUB = 16
HELD = ZL // CN
BF, F32 = jnp.bfloat16, jnp.float32


def nt(a, b):
    return lax.dot_general(a, b, (((1,), (1,)), ((), ())), preferred_element_type=F32)


def attend_kernel(length_ref, q_ref, k_ref, v_ref, g_ref, _, vg_ref, kg_ref):
    scaling = HD ** (-0.5)
    keys, vals = k_ref[...], v_ref[...]
    length = length_ref[0]
    step = 2
    wide = step * TOK
    pos_s = lax.broadcasted_iota(jnp.int32, (TOK, wide), 0)
    pos_t = lax.broadcasted_iota(jnp.int32, (TOK, wide), 1) & (TOK - 1)
    allowed = pos_s <= pos_t
    live = ((lax.broadcasted_iota(jnp.int32, (1, wide), 1) & (TOK - 1)) < length).astype(F32)
    vg = jnp.zeros((TOK, HD), F32)
    kg = jnp.zeros((TOK, HD), F32)
    for first in range(0, GROUP, step):
        heads = range(first, first + step)
        qs = jnp.concatenate([q_ref[:, h * HD : (h + 1) * HD] for h in heads], axis=0)
        gs = jnp.concatenate([g_ref[:, h * HD : (h + 1) * HD] for h in heads], axis=0)
        scores = jnp.where(allowed, nt(keys, qs) * scaling, F32(-1e30))
        expd = jnp.exp(scores - jnp.max(scores, axis=0, keepdims=True))
        probs = expd * (live / jnp.sum(expd, axis=0, keepdims=True))
        dprob = nt(vals, gs)
        delta = jnp.sum(probs * dprob, axis=0, keepdims=True)
        dscore = probs * (dprob - delta)
        vg += jnp.dot(probs.astype(BF), gs, preferred_element_type=F32)
        kg += jnp.dot(dscore.astype(BF), qs, preferred_element_type=F32)
    vg_ref[...] = vg.astype(BF)
    kg_ref[...] = (kg * scaling).astype(BF)


def attend_back(query, key_rows, value_rows, grad_rows, length, earlier):
    heads = KV // HD
    wide = pl.BlockSpec((TOK, GROUP * HD), lambda g: (0, g))
    thin = pl.BlockSpec((TOK, HD), lambda g: (0, g))
    return pl.pallas_call(
        attend_kernel,
        grid=(heads,),
        in_specs=[pl.BlockSpec(memory_space=pltpu.SMEM), wide, thin, thin, wide, pl.BlockSpec(memory_space=pl.ANY)],
        out_specs=[thin, thin],
        out_shape=[jax.ShapeDtypeStruct((TOK, KV), BF)] * 2,
        cost_estimate=pl.CostEstimate(
            flops=10 * 32 * TOK * TOK * HD, bytes_accessed=3 << 20, transcendentals=32 * TOK * TOK
        ),
        name="attend",
    )(length, query, key_rows, value_rows, grad_rows, earlier)


def swap_groups(tiles):
    lane = lax.broadcasted_iota(jnp.int32, tiles[0].shape, 1)
    for bit in (1, 2, 4):
        shift = bit * SUB
        high = (lane & shift) != 0
        after = list(tiles)
        for i in range(8):
            if i & bit == 0:
                low_tile, high_tile = tiles[i], tiles[i | bit]
                after[i] = jnp.where(high, pltpu.roll(high_tile, shift, 1), low_tile)
                after[i | bit] = jnp.where(high, high_tile, pltpu.roll(low_tile, 128 - shift, 1))
        tiles = after
    return tiles


def to_pieces_kernel(in_ref, out_ref):
    for x in range(XN):
        tiles = [in_ref[:, (zl * XN + x) * 128 : (zl * XN + x + 1) * 128].astype(F32) for zl in range(8)]
        for q, tile in enumerate(swap_groups(tiles)):
            y = q % YN
            out_ref[q // YN * XN + x, :, y * 128 : (y + 1) * 128] = tile.astype(BF)


def from_pieces_kernel(at_ref, *refs):
    out_ref = refs[-1]
    for by in range(XN):
        x = (at_ref[2] + XN - by) % XN
        for which in range(CN):
            for k in range(HELD):
                tile = (at_ref[which] + ZL - k) % ZL * XN + x
                lanes = pl.ds(pl.multiple_of(tile * 128, 128), 128)
                out_ref[:, lanes] = refs[by][which, :, k * 128 : (k + 1) * 128]


def to_pieces(rows):
    part = 32
    return pl.pallas_call(
        to_pieces_kernel,
        grid=(TOK // part,),
        in_specs=[pl.BlockSpec((part, WIDTH), lambda i: (i, 0))],
        out_specs=pl.BlockSpec((QN, part, KV), lambda i: (0, i, 0)),
        out_shape=jax.ShapeDtypeStruct((QN, TOK, KV), BF),
        cost_estimate=pl.CostEstimate(flops=1 << 22, bytes_accessed=2 << 20, transcendentals=0),
        name="to_pieces",
    )(rows)


def from_pieces(pieces, core, zl, x):
    part = 32
    firsts = [(zl + ZL - HELD * c) % ZL for c in (core, 1 - core)]
    return pl.pallas_call(
        from_pieces_kernel,
        grid=(TOK // part,),
        in_specs=[pl.BlockSpec(memory_space=pltpu.SMEM)]
        + [pl.BlockSpec((CN, part, KV), lambda i: (0, i, 0))] * XN,
        out_specs=pl.BlockSpec((part, WIDTH), lambda i: (i, 0)),
        out_shape=jax.ShapeDtypeStruct((TOK, WIDTH), BF),
        cost_estimate=pl.CostEstimate(flops=0, bytes_accessed=2 << 20, transcendentals=0),
        compiler_params=pltpu.CompilerParams(vmem_limit_bytes=16 << 20),
        name="from_pieces",
    )(jnp.stack(firsts + [x]).astype(jnp.int32), *pieces)


def exchange(array, axes):
    return lax.all_to_all(array, axes, 0, 0, tiled=True)


def spread(array, axes, count):
    return exchange(jnp.broadcast_to(array[None], (count,) + array.shape), axes)


def shifted(array, axes, count, by):
    return lax.ppermute(array, axes, [(i, (i + by) % count) for i in range(count)])


def along_z(array, steps):
    pairs = []
    for z in range(ZH * ZL):
        for core, by in enumerate(steps):
            to = (z + by) % (ZH * ZL)
            pairs.append((((z % ZL) * ZH + z // ZL) * CN + core, ((to % ZL) * ZH + to // ZL) * CN + core))
    return lax.ppermute(array, ("zl", "zh", "core"), pairs)


def pair_kernel(core_ref, own_ref, other_ref, out_ref):
    core = core_ref[0]
    out_ref[core] = own_ref[...]
    out_ref[1 - core] = other_ref[...]


def pair(own, other, core):
    vmem = pl.BlockSpec(memory_space=pltpu.VMEM)
    return pl.pallas_call(
        pair_kernel,
        in_specs=[pl.BlockSpec(memory_space=pltpu.SMEM), vmem, vmem],
        out_specs=vmem,
        out_shape=jax.ShapeDtypeStruct((CN,) + own.shape, own.dtype),
        compiler_params=pltpu.CompilerParams(vmem_limit_bytes=16 << 20),
        name="pair",
    )(core[None].astype(jnp.int32), own, other)


def join_kernel(*refs):
    out_ref = refs[-1]
    for i, ref in enumerate(refs[:-2]):
        out_ref[i * 128 : (i + 1) * 128, :] = ref[...]


def join(blocks, earlier):
    vmem = pl.BlockSpec(memory_space=pltpu.VMEM)
    return pl.pallas_call(
        join_kernel,
        in_specs=[vmem] * len(blocks) + [pl.BlockSpec(memory_space=pl.ANY)],
        out_specs=vmem,
        out_shape=jax.ShapeDtypeStruct((len(blocks) * 128, KV), BF),
        compiler_params=pltpu.CompilerParams(vmem_limit_bytes=16 << 20),
        name="join",
    )(*blocks, earlier)


def per_device(inputs, queries, keys, values, out_grad, lengths, value_weight):
    core, x, zl = (lax.axis_index(name) for name in ("core", "x", "zl"))
    with jax.named_scope("cut_inputs"):
        pieces = to_pieces(inputs[0])
    with jax.named_scope("attention"):
        value_grad, key_grad = attend_back(queries[0], keys[0], values[0], out_grad[0], lengths, pieces)
    with jax.named_scope("gather_value_grad"):
        mine = lax.all_gather(value_grad, "x", axis=0)
        other = shifted(mine, "core", CN, 1)
        grads = pair(mine, other, core).reshape(CN * XN * TOK, KV)
    with jax.named_scope("send_inputs"):
        columns = exchange(pieces, ("core", "x"))
    with jax.named_scope("weight_term"):
        term = lax.dot_general(
            columns.reshape(CN * XN * TOK, KV), grads, (((0,), (0,)), ((), ())), preferred_element_type=F32
        ).astype(BF)
    with jax.named_scope("sum_y"):
        got = exchange(term.reshape(YN, ZL * SUB, KV), "y")
        plane = jnp.sum(got.astype(F32), axis=0).astype(BF).reshape(1, ZL, SUB, KV)
    with jax.named_scope("sum_z"):
        both = jnp.broadcast_to(plane, (ZH, ZL, SUB, KV)).reshape(ZH * ZL, SUB, KV)
        got = exchange(both, ("zh", "zl"))
        total = jnp.sum(got.astype(F32), axis=0) * F32(1.0 / 512)
    with jax.named_scope("share_rows"):
        weight_grad = spread(total.astype(BF), ("core", "y"), QN).reshape(QN * SUB, KV).astype(F32)
    with jax.named_scope("gather_weight"):
        weight = join([along_z(value_weight, steps) for steps in ((0, 4), (1, -3), (2, -2), (3, -1))], plane)
    with jax.named_scope("input_grad"):
        parts = nt(grads, weight).astype(BF).reshape(CN, XN, TOK, KV)
        kept = lax.dynamic_index_in_dim(parts, core, 0, False)
        theirs = shifted(lax.dynamic_index_in_dim(parts, 1 - core, 0, False), "core", CN, 1)
        parts = jnp.stack([kept, theirs], axis=1)
        back = []
        for by in range(XN):
            piece = lax.dynamic_index_in_dim(parts, (x + by) % XN, 0, False)
            back.append(shifted(piece, "x", XN, by) if by else piece)
        input_grad = from_pieces(back, core, zl, x)
    return (input_grad[None], key_grad[None], weight_grad)


def solution(mesh):
    names = ("zl", "x", "y", "zh", "core")
    fine = Mesh(mesh.devices.reshape(ZL, XN, YN, ZH, CN), names)
    blk = names[:2]
    rows = P(names, None, None)
    return jax.shard_map(
        per_device,
        mesh=fine,
        in_specs=(rows, rows, rows, rows, rows, P(names), P(blk, None)),
        out_specs=(rows, rows, P(blk, None)),
        check_vma=False,
    )
```

```python
import jax
import jax.numpy as jnp
from jax import lax
from jax.experimental import pallas as pl
from jax.experimental.pallas import tpu as pltpu
from jax.sharding import Mesh
from jax.sharding import PartitionSpec as P

ZL, XN, YN, ZH, CN = 8, 4, 4, 2, 2
QN = CN * YN
TOK, WIDTH, KV, HD = 128, 4096, 512, 128
GROUP = 8
KV_STEP = 2
SUB = 16
HELD = ZL // CN
BF, F32 = jnp.bfloat16, jnp.float32


def nt(a, b):
    return lax.dot_general(a, b, (((1,), (1,)), ((), ())), preferred_element_type=F32)


def attend_kernel(length_ref, q_ref, k_ref, v_ref, g_ref, _, vg_ref, kg_ref):
    scaling = HD ** (-0.5)
    length = length_ref[0]
    wide = GROUP * TOK
    pos_s = lax.broadcasted_iota(jnp.int32, (TOK, wide), 0)
    pos_t = lax.broadcasted_iota(jnp.int32, (TOK, wide), 1) & (TOK - 1)
    allowed = pos_s <= pos_t
    live = ((lax.broadcasted_iota(jnp.int32, (1, wide), 1) & (TOK - 1)) < length).astype(F32)
    for head in range(KV_STEP):
        cols = slice(head * HD, (head + 1) * HD)
        heads = range(head * GROUP, (head + 1) * GROUP)
        qs = jnp.concatenate([q_ref[:, h * HD : (h + 1) * HD] for h in heads], axis=0)
        gs = jnp.concatenate([g_ref[:, h * HD : (h + 1) * HD] for h in heads], axis=0)
        scores = jnp.where(allowed, nt(k_ref[:, cols], qs) * scaling, F32(-1e30))
        expd = jnp.exp(scores - jnp.max(scores, axis=0, keepdims=True))
        probs = expd * (live / jnp.sum(expd, axis=0, keepdims=True))
        dprob = nt(v_ref[:, cols], gs)
        delta = jnp.sum(probs * dprob, axis=0, keepdims=True)
        dscore = probs * (dprob - delta)
        vg = jnp.dot(probs.astype(BF), gs, preferred_element_type=F32)
        kg = jnp.dot(dscore.astype(BF), qs, preferred_element_type=F32)
        vg_ref[:, cols] = vg.astype(BF)
        kg_ref[:, cols] = (kg * scaling).astype(BF)


def attend_back(query, key_rows, value_rows, grad_rows, length, earlier):
    wide = pl.BlockSpec((TOK, KV_STEP * GROUP * HD), lambda g: (0, g))
    thin = pl.BlockSpec((TOK, KV_STEP * HD), lambda g: (0, g))
    return pl.pallas_call(
        attend_kernel,
        grid=(KV // HD // KV_STEP,),
        in_specs=[pl.BlockSpec(memory_space=pltpu.SMEM), wide, thin, thin, wide, pl.BlockSpec(memory_space=pl.ANY)],
        out_specs=[thin, thin],
        out_shape=[jax.ShapeDtypeStruct((TOK, KV), BF)] * 2,
        cost_estimate=pl.CostEstimate(
            flops=10 * 32 * TOK * TOK * HD, bytes_accessed=3 << 20, transcendentals=32 * TOK * TOK
        ),
        name="attend",
    )(length, query, key_rows, value_rows, grad_rows, earlier)


def swap_groups(tiles):
    lane = lax.broadcasted_iota(jnp.int32, tiles[0].shape, 1)
    for bit in (1, 2, 4):
        shift = bit * SUB
        high = (lane & shift) != 0
        after = list(tiles)
        for i in range(8):
            if i & bit == 0:
                low_tile, high_tile = tiles[i], tiles[i | bit]
                after[i] = jnp.where(high, pltpu.roll(high_tile, shift, 1), low_tile)
                after[i | bit] = jnp.where(high, high_tile, pltpu.roll(low_tile, 128 - shift, 1))
        tiles = after
    return tiles


def to_pieces_kernel(in_ref, out_ref):
    for x in range(XN):
        tiles = [in_ref[:, (zl * XN + x) * 128 : (zl * XN + x + 1) * 128].astype(F32) for zl in range(8)]
        for q, tile in enumerate(swap_groups(tiles)):
            y = q % YN
            out_ref[q // YN * XN + x, :, y * 128 : (y + 1) * 128] = tile.astype(BF)


def from_pieces_kernel(at_ref, *refs):
    out_ref = refs[-1]
    for by in range(XN):
        x = (at_ref[2] + XN - by) % XN
        for which in range(CN):
            for k in range(HELD):
                tile = (at_ref[which] + ZL - k) % ZL * XN + x
                lanes = pl.ds(pl.multiple_of(tile * 128, 128), 128)
                out_ref[:, lanes] = refs[by][which, :, k * 128 : (k + 1) * 128]


def to_pieces(rows):
    part = 64
    return pl.pallas_call(
        to_pieces_kernel,
        grid=(TOK // part,),
        in_specs=[pl.BlockSpec((part, WIDTH), lambda i: (i, 0))],
        out_specs=pl.BlockSpec((QN, part, KV), lambda i: (0, i, 0)),
        out_shape=jax.ShapeDtypeStruct((QN, TOK, KV), BF),
        cost_estimate=pl.CostEstimate(flops=1 << 22, bytes_accessed=2 << 20, transcendentals=0),
        name="to_pieces",
    )(rows)


def from_pieces(pieces, core, zl, x):
    part = 64
    firsts = [(zl + ZL - HELD * c) % ZL for c in (core, 1 - core)]
    return pl.pallas_call(
        from_pieces_kernel,
        grid=(TOK // part,),
        in_specs=[pl.BlockSpec(memory_space=pltpu.SMEM)]
        + [pl.BlockSpec((CN, part, KV), lambda i: (0, i, 0))] * XN,
        out_specs=pl.BlockSpec((part, WIDTH), lambda i: (i, 0)),
        out_shape=jax.ShapeDtypeStruct((TOK, WIDTH), BF),
        cost_estimate=pl.CostEstimate(flops=0, bytes_accessed=2 << 20, transcendentals=0),
        compiler_params=pltpu.CompilerParams(vmem_limit_bytes=16 << 20),
        name="from_pieces",
    )(jnp.stack(firsts + [x]).astype(jnp.int32), *pieces)


def exchange(array, axes):
    return lax.all_to_all(array, axes, 0, 0, tiled=True)


def spread(array, axes, count):
    return exchange(jnp.broadcast_to(array[None], (count,) + array.shape), axes)


def shifted(array, axes, count, by):
    return lax.ppermute(array, axes, [(i, (i + by) % count) for i in range(count)])


def along_z(array, steps):
    pairs = []
    for z in range(ZH * ZL):
        for core, by in enumerate(steps):
            to = (z + by) % (ZH * ZL)
            pairs.append((((z % ZL) * ZH + z // ZL) * CN + core, ((to % ZL) * ZH + to // ZL) * CN + core))
    return lax.ppermute(array, ("zl", "zh", "core"), pairs)


def pair_kernel(core_ref, own_ref, other_ref, out_ref):
    core = core_ref[0]
    out_ref[core] = own_ref[...]
    out_ref[1 - core] = other_ref[...]


def pair(own, other, core):
    vmem = pl.BlockSpec(memory_space=pltpu.VMEM)
    return pl.pallas_call(
        pair_kernel,
        in_specs=[pl.BlockSpec(memory_space=pltpu.SMEM), vmem, vmem],
        out_specs=vmem,
        out_shape=jax.ShapeDtypeStruct((CN,) + own.shape, own.dtype),
        compiler_params=pltpu.CompilerParams(vmem_limit_bytes=16 << 20),
        name="pair",
    )(core[None].astype(jnp.int32), own, other)


def join_kernel(*refs):
    out_ref = refs[-1]
    for i, ref in enumerate(refs[:-2]):
        out_ref[i * 128 : (i + 1) * 128, :] = ref[...]


def join(blocks, earlier):
    vmem = pl.BlockSpec(memory_space=pltpu.VMEM)
    return pl.pallas_call(
        join_kernel,
        in_specs=[vmem] * len(blocks) + [pl.BlockSpec(memory_space=pl.ANY)],
        out_specs=vmem,
        out_shape=jax.ShapeDtypeStruct((len(blocks) * 128, KV), BF),
        compiler_params=pltpu.CompilerParams(vmem_limit_bytes=16 << 20),
        name="join",
    )(*blocks, earlier)


def per_device(inputs, queries, keys, values, out_grad, lengths, value_weight):
    core, x, zl = (lax.axis_index(name) for name in ("core", "x", "zl"))
    with jax.named_scope("cut_inputs"):
        pieces = to_pieces(inputs[0])
    with jax.named_scope("attention"):
        value_grad, key_grad = attend_back(queries[0], keys[0], values[0], out_grad[0], lengths, pieces)
    with jax.named_scope("gather_value_grad"):
        mine = lax.all_gather(value_grad, "x", axis=0)
        other = shifted(mine, "core", CN, 1)
        grads = pair(mine, other, core).reshape(CN * XN * TOK, KV)
    with jax.named_scope("send_inputs"):
        columns = exchange(pieces, ("core", "x"))
    with jax.named_scope("weight_term"):
        term = lax.dot_general(
            columns.reshape(CN * XN * TOK, KV), grads, (((0,), (0,)), ((), ())), preferred_element_type=F32
        ).astype(BF)
    with jax.named_scope("sum_y"):
        got = exchange(term.reshape(YN, ZL * SUB, KV), "y")
        plane = jnp.sum(got.astype(F32), axis=0).astype(BF).reshape(1, ZL, SUB, KV)
    with jax.named_scope("sum_z"):
        both = jnp.broadcast_to(plane, (ZH, ZL, SUB, KV)).reshape(ZH * ZL, SUB, KV)
        got = exchange(both, ("zh", "zl"))
        total = jnp.sum(got.astype(F32), axis=0) * F32(1.0 / 512)
    with jax.named_scope("share_rows"):
        weight_grad = spread(total.astype(BF), ("core", "y"), QN).reshape(QN * SUB, KV).astype(F32)
    with jax.named_scope("gather_weight"):
        weight = join([along_z(value_weight, steps) for steps in ((0, 4), (1, -3), (2, -2), (3, -1))], plane)
    with jax.named_scope("input_grad"):
        parts = nt(grads, weight).astype(BF).reshape(CN, XN, TOK, KV)
        kept = lax.dynamic_index_in_dim(parts, core, 0, False)
        theirs = shifted(lax.dynamic_index_in_dim(parts, 1 - core, 0, False), "core", CN, 1)
        parts = jnp.stack([kept, theirs], axis=1)
        back = []
        for by in range(XN):
            piece = lax.dynamic_index_in_dim(parts, (x + by) % XN, 0, False)
            back.append(shifted(piece, "x", XN, by) if by else piece)
        input_grad = from_pieces(back, core, zl, x)
    return (input_grad[None], key_grad[None], weight_grad)


def solution(mesh):
    names = ("zl", "x", "y", "zh", "core")
    fine = Mesh(mesh.devices.reshape(ZL, XN, YN, ZH, CN), names)
    blk = names[:2]
    rows = P(names, None, None)
    return jax.shard_map(
        per_device,
        mesh=fine,
        in_specs=(rows, rows, rows, rows, rows, P(names), P(blk, None)),
        out_specs=(rows, rows, P(blk, None)),
        check_vma=False,
    )
```

```python
import jax
import jax.numpy as jnp
from jax import lax
from jax.experimental import pallas as pl
from jax.experimental.pallas import tpu as pltpu
from jax.sharding import Mesh
from jax.sharding import PartitionSpec as P

ZL, XN, YN, ZH, CN = 8, 4, 4, 2, 2
QN = CN * YN
TOK, WIDTH, KV, HD = 128, 4096, 512, 128
GROUP = 8
KV_STEP = 2
SUB = 16
HELD = ZL // CN
BF, F32 = jnp.bfloat16, jnp.float32


def nt(a, b):
    return lax.dot_general(a, b, (((1,), (1,)), ((), ())), preferred_element_type=F32)


def attend_kernel(length_ref, q_ref, k_ref, v_ref, g_ref, _, vg_ref, kg_ref):
    scaling = HD ** (-0.5)
    length = length_ref[0]
    wide = GROUP * TOK
    pos_s = lax.broadcasted_iota(jnp.int32, (TOK, wide), 0)
    pos_t = lax.broadcasted_iota(jnp.int32, (TOK, wide), 1) & (TOK - 1)
    allowed = pos_s <= pos_t
    live = ((lax.broadcasted_iota(jnp.int32, (1, wide), 1) & (TOK - 1)) < length).astype(F32)
    for head in range(KV_STEP):
        cols = slice(head * HD, (head + 1) * HD)
        heads = range(head * GROUP, (head + 1) * GROUP)
        qs = jnp.concatenate([q_ref[:, h * HD : (h + 1) * HD] for h in heads], axis=0)
        gs = jnp.concatenate([g_ref[:, h * HD : (h + 1) * HD] for h in heads], axis=0)
        scores = jnp.where(allowed, nt(k_ref[:, cols], qs) * scaling, F32(-1e30))
        expd = jnp.exp(scores - jnp.max(scores, axis=0, keepdims=True))
        probs = expd * (live / jnp.sum(expd, axis=0, keepdims=True))
        dprob = nt(v_ref[:, cols], gs)
        delta = jnp.sum(probs * dprob, axis=0, keepdims=True)
        dscore = probs * (dprob - delta)
        vg = jnp.dot(probs.astype(BF), gs, preferred_element_type=F32)
        kg = jnp.dot(dscore.astype(BF), qs, preferred_element_type=F32)
        vg_ref[:, cols] = vg.astype(BF)
        kg_ref[:, cols] = (kg * scaling).astype(BF)


def attend_back(query, key_rows, value_rows, grad_rows, length, earlier):
    wide = pl.BlockSpec((TOK, KV_STEP * GROUP * HD), lambda g: (0, g))
    thin = pl.BlockSpec((TOK, KV_STEP * HD), lambda g: (0, g))
    return pl.pallas_call(
        attend_kernel,
        grid=(KV // HD // KV_STEP,),
        in_specs=[pl.BlockSpec(memory_space=pltpu.SMEM), wide, thin, thin, wide, pl.BlockSpec(memory_space=pl.ANY)],
        out_specs=[thin, thin],
        out_shape=[jax.ShapeDtypeStruct((TOK, KV), BF)] * 2,
        cost_estimate=pl.CostEstimate(
            flops=10 * 32 * TOK * TOK * HD, bytes_accessed=3 << 20, transcendentals=32 * TOK * TOK
        ),
        name="attend",
    )(length, query, key_rows, value_rows, grad_rows, earlier)


def swap_groups(tiles):
    lane = lax.broadcasted_iota(jnp.int32, tiles[0].shape, 1)
    for bit in (1, 2, 4):
        shift = bit * SUB
        high = (lane & shift) != 0
        after = list(tiles)
        for i in range(8):
            if i & bit == 0:
                low_tile, high_tile = tiles[i], tiles[i | bit]
                after[i] = jnp.where(high, pltpu.roll(high_tile, shift, 1), low_tile)
                after[i | bit] = jnp.where(high, high_tile, pltpu.roll(low_tile, 128 - shift, 1))
        tiles = after
    return tiles


def to_pieces_kernel(in_ref, out_ref):
    for x in range(XN):
        tiles = [in_ref[:, (zl * XN + x) * 128 : (zl * XN + x + 1) * 128].astype(F32) for zl in range(8)]
        for q, tile in enumerate(swap_groups(tiles)):
            y = q % YN
            out_ref[q // YN * XN + x, :, y * 128 : (y + 1) * 128] = tile.astype(BF)


def from_pieces_kernel(at_ref, *refs):
    out_ref = refs[-1]
    for by in range(XN):
        x = (at_ref[2] + XN - by) % XN
        for which in range(CN):
            for k in range(HELD):
                tile = (at_ref[which] + ZL - k) % ZL * XN + x
                lanes = pl.ds(pl.multiple_of(tile * 128, 128), 128)
                out_ref[:, lanes] = refs[by][which, :, k * 128 : (k + 1) * 128]


def to_pieces(rows):
    part = 64
    return pl.pallas_call(
        to_pieces_kernel,
        grid=(TOK // part,),
        in_specs=[pl.BlockSpec((part, WIDTH), lambda i: (i, 0))],
        out_specs=pl.BlockSpec((QN, part, KV), lambda i: (0, i, 0)),
        out_shape=jax.ShapeDtypeStruct((QN, TOK, KV), BF),
        cost_estimate=pl.CostEstimate(flops=1 << 22, bytes_accessed=2 << 20, transcendentals=0),
        name="to_pieces",
    )(rows)


def from_pieces(pieces, core, zl, x):
    part = 64
    firsts = [(zl + ZL - HELD * c) % ZL for c in (core, 1 - core)]
    return pl.pallas_call(
        from_pieces_kernel,
        grid=(TOK // part,),
        in_specs=[pl.BlockSpec(memory_space=pltpu.SMEM)]
        + [pl.BlockSpec((CN, part, KV), lambda i: (0, i, 0))] * XN,
        out_specs=pl.BlockSpec((part, WIDTH), lambda i: (i, 0)),
        out_shape=jax.ShapeDtypeStruct((TOK, WIDTH), BF),
        cost_estimate=pl.CostEstimate(flops=0, bytes_accessed=2 << 20, transcendentals=0),
        compiler_params=pltpu.CompilerParams(vmem_limit_bytes=16 << 20),
        name="from_pieces",
    )(jnp.stack(firsts + [x]).astype(jnp.int32), *pieces)


def exchange(array, axes):
    return lax.all_to_all(array, axes, 0, 0, tiled=True)


def spread(array, axes, count):
    return exchange(jnp.broadcast_to(array[None], (count,) + array.shape), axes)


def shifted(array, axes, count, by):
    return lax.ppermute(array, axes, [(i, (i + by) % count) for i in range(count)])


def along_z(array, steps):
    pairs = []
    for z in range(ZH * ZL):
        for core, by in enumerate(steps):
            to = (z + by) % (ZH * ZL)
            pairs.append((((z % ZL) * ZH + z // ZL) * CN + core, ((to % ZL) * ZH + to // ZL) * CN + core))
    return lax.ppermute(array, ("zl", "zh", "core"), pairs)


def hold_kernel(in_ref, *refs):
    refs[-1][...] = in_ref[...]


def hold(array, earlier):
    vmem = pl.BlockSpec(memory_space=pltpu.VMEM)
    return pl.pallas_call(
        hold_kernel,
        in_specs=[vmem] + [pl.BlockSpec(memory_space=pl.ANY)] * len(earlier),
        out_specs=vmem,
        out_shape=jax.ShapeDtypeStruct(array.shape, array.dtype),
        compiler_params=pltpu.CompilerParams(vmem_limit_bytes=16 << 20),
        name="hold",
    )(array, *earlier)


def pair_kernel(core_ref, own_ref, other_ref, out_ref):
    core = core_ref[0]
    out_ref[core] = own_ref[...]
    out_ref[1 - core] = other_ref[...]


def pair(own, other, core):
    vmem = pl.BlockSpec(memory_space=pltpu.VMEM)
    return pl.pallas_call(
        pair_kernel,
        in_specs=[pl.BlockSpec(memory_space=pltpu.SMEM), vmem, vmem],
        out_specs=vmem,
        out_shape=jax.ShapeDtypeStruct((CN,) + own.shape, own.dtype),
        compiler_params=pltpu.CompilerParams(vmem_limit_bytes=16 << 20),
        name="pair",
    )(core[None].astype(jnp.int32), own, other)


def join_kernel(*refs):
    out_ref = refs[-1]
    for i, ref in enumerate(refs[:-2]):
        out_ref[i * 128 : (i + 1) * 128, :] = ref[...]


def join(blocks, earlier):
    vmem = pl.BlockSpec(memory_space=pltpu.VMEM)
    return pl.pallas_call(
        join_kernel,
        in_specs=[vmem] * len(blocks) + [pl.BlockSpec(memory_space=pl.ANY)],
        out_specs=vmem,
        out_shape=jax.ShapeDtypeStruct((len(blocks) * 128, KV), BF),
        compiler_params=pltpu.CompilerParams(vmem_limit_bytes=16 << 20),
        name="join",
    )(*blocks, earlier)


def per_device(inputs, queries, keys, values, out_grad, lengths, value_weight):
    core, x, zl = (lax.axis_index(name) for name in ("core", "x", "zl"))
    with jax.named_scope("cut_inputs"):
        pieces = to_pieces(inputs[0])
    with jax.named_scope("attention"):
        value_grad, key_grad = attend_back(queries[0], keys[0], values[0], out_grad[0], lengths, pieces)
    with jax.named_scope("gather_value_grad"):
        near = [along_z(value_weight, steps) for steps in ((1, -3), (2, -2))]
        mine = hold(lax.all_gather(value_grad, "x", axis=0), near)
        other = shifted(mine, "core", CN, 1)
        grads = pair(mine, other, core).reshape(CN * XN * TOK, KV)
    with jax.named_scope("send_inputs"):
        columns = exchange(pieces, ("core", "x"))
    with jax.named_scope("weight_term"):
        term = lax.dot_general(
            columns.reshape(CN * XN * TOK, KV), grads, (((0,), (0,)), ((), ())), preferred_element_type=F32
        ).astype(BF)
    with jax.named_scope("sum_y"):
        got = exchange(term.reshape(YN, ZL * SUB, KV), "y")
        plane = jnp.sum(got.astype(F32), axis=0).astype(BF).reshape(1, ZL, SUB, KV)
    with jax.named_scope("sum_z"):
        both = jnp.broadcast_to(plane, (ZH, ZL, SUB, KV)).reshape(ZH * ZL, SUB, KV)
        got = exchange(both, ("zh", "zl"))
        total = jnp.sum(got.astype(F32), axis=0) * F32(1.0 / 512)
    with jax.named_scope("share_rows"):
        weight_grad = spread(total.astype(BF), ("core", "y"), QN).reshape(QN * SUB, KV).astype(F32)
    with jax.named_scope("gather_weight"):
        first, last = (along_z(value_weight, steps) for steps in ((0, 4), (3, -1)))
        weight = join([first] + near + [last], plane)
    with jax.named_scope("input_grad"):
        parts = nt(grads, weight).astype(BF).reshape(CN, XN, TOK, KV)
        kept = lax.dynamic_index_in_dim(parts, core, 0, False)
        theirs = shifted(lax.dynamic_index_in_dim(parts, 1 - core, 0, False), "core", CN, 1)
        parts = jnp.stack([kept, theirs], axis=1)
        back = []
        for by in range(XN):
            piece = lax.dynamic_index_in_dim(parts, (x + by) % XN, 0, False)
            back.append(shifted(piece, "x", XN, by) if by else piece)
        input_grad = from_pieces(back, core, zl, x)
    return (input_grad[None], key_grad[None], weight_grad)


def solution(mesh):
    names = ("zl", "x", "y", "zh", "core")
    fine = Mesh(mesh.devices.reshape(ZL, XN, YN, ZH, CN), names)
    blk = names[:2]
    rows = P(names, None, None)
    return jax.shard_map(
        per_device,
        mesh=fine,
        in_specs=(rows, rows, rows, rows, rows, P(names), P(blk, None)),
        out_specs=(rows, rows, P(blk, None)),
        check_vma=False,
    )
```

```python
import jax
import jax.numpy as jnp
from jax import lax
from jax.experimental import pallas as pl
from jax.experimental.pallas import tpu as pltpu
from jax.sharding import Mesh
from jax.sharding import PartitionSpec as P

ZL, XN, YN, ZH, CN = 8, 4, 4, 2, 2
QN = CN * YN
TOK, WIDTH, KV, HD = 128, 4096, 512, 128
GROUP = 8
KV_STEP = 2
SUB = 16
HELD = ZL // CN
BF, F32 = jnp.bfloat16, jnp.float32


def nt(a, b):
    return lax.dot_general(a, b, (((1,), (1,)), ((), ())), preferred_element_type=F32)


def attend_kernel(length_ref, q_ref, k_ref, v_ref, g_ref, _, vg_ref, kg_ref):
    scaling = HD ** (-0.5)
    length = length_ref[0]
    wide = GROUP * TOK
    pos_s = lax.broadcasted_iota(jnp.int32, (TOK, wide), 0)
    pos_t = lax.broadcasted_iota(jnp.int32, (TOK, wide), 1) & (TOK - 1)
    allowed = pos_s <= pos_t
    live = ((lax.broadcasted_iota(jnp.int32, (1, wide), 1) & (TOK - 1)) < length).astype(F32)
    for head in range(KV_STEP):
        cols = slice(head * HD, (head + 1) * HD)
        heads = range(head * GROUP, (head + 1) * GROUP)
        qs = jnp.concatenate([q_ref[:, h * HD : (h + 1) * HD] for h in heads], axis=0)
        gs = jnp.concatenate([g_ref[:, h * HD : (h + 1) * HD] for h in heads], axis=0)
        scores = jnp.where(allowed, nt(k_ref[:, cols], qs) * scaling, F32(-1e30))
        expd = jnp.exp(scores - jnp.max(scores, axis=0, keepdims=True))
        probs = expd * (live / jnp.sum(expd, axis=0, keepdims=True))
        dprob = nt(v_ref[:, cols], gs)
        delta = jnp.sum(probs * dprob, axis=0, keepdims=True)
        dscore = probs * (dprob - delta)
        vg = jnp.dot(probs.astype(BF), gs, preferred_element_type=F32)
        kg = jnp.dot(dscore.astype(BF), qs, preferred_element_type=F32)
        vg_ref[:, cols] = vg.astype(BF)
        kg_ref[:, cols] = (kg * scaling).astype(BF)


def attend_back(query, key_rows, value_rows, grad_rows, length, earlier):
    wide = pl.BlockSpec((TOK, KV_STEP * GROUP * HD), lambda g: (0, g))
    thin = pl.BlockSpec((TOK, KV_STEP * HD), lambda g: (0, g))
    return pl.pallas_call(
        attend_kernel,
        grid=(KV // HD // KV_STEP,),
        in_specs=[pl.BlockSpec(memory_space=pltpu.SMEM), wide, thin, thin, wide, pl.BlockSpec(memory_space=pl.ANY)],
        out_specs=[thin, thin],
        out_shape=[jax.ShapeDtypeStruct((TOK, KV), BF)] * 2,
        cost_estimate=pl.CostEstimate(
            flops=10 * 32 * TOK * TOK * HD, bytes_accessed=3 << 20, transcendentals=32 * TOK * TOK
        ),
        name="attend",
    )(length, query, key_rows, value_rows, grad_rows, earlier)


def swap_groups(tiles):
    lane = lax.broadcasted_iota(jnp.int32, tiles[0].shape, 1)
    for bit in (1, 2, 4):
        shift = bit * SUB
        high = (lane & shift) != 0
        after = list(tiles)
        for i in range(8):
            if i & bit == 0:
                low_tile, high_tile = tiles[i], tiles[i | bit]
                after[i] = jnp.where(high, pltpu.roll(high_tile, shift, 1), low_tile)
                after[i | bit] = jnp.where(high, high_tile, pltpu.roll(low_tile, 128 - shift, 1))
        tiles = after
    return tiles


def to_pieces_kernel(in_ref, out_ref):
    for x in range(XN):
        tiles = [in_ref[:, (zl * XN + x) * 128 : (zl * XN + x + 1) * 128].astype(F32) for zl in range(8)]
        for q, tile in enumerate(swap_groups(tiles)):
            y = q % YN
            out_ref[q // YN * XN + x, :, y * 128 : (y + 1) * 128] = tile.astype(BF)


def from_pieces_kernel(at_ref, *refs):
    out_ref = refs[-1]
    for by in range(XN):
        x = (at_ref[2] + XN - by) % XN
        for which in range(CN):
            for k in range(HELD):
                tile = (at_ref[which] + ZL - k) % ZL * XN + x
                lanes = pl.ds(pl.multiple_of(tile * 128, 128), 128)
                out_ref[:, lanes] = refs[by][which, :, k * 128 : (k + 1) * 128]


def to_pieces(rows):
    part = 64
    return pl.pallas_call(
        to_pieces_kernel,
        grid=(TOK // part,),
        in_specs=[pl.BlockSpec((part, WIDTH), lambda i: (i, 0))],
        out_specs=pl.BlockSpec((QN, part, KV), lambda i: (0, i, 0)),
        out_shape=jax.ShapeDtypeStruct((QN, TOK, KV), BF),
        cost_estimate=pl.CostEstimate(flops=1 << 22, bytes_accessed=2 << 20, transcendentals=0),
        name="to_pieces",
    )(rows)


def from_pieces(pieces, core, zl, x):
    part = 64
    firsts = [(zl + ZL - HELD * c) % ZL for c in (core, 1 - core)]
    return pl.pallas_call(
        from_pieces_kernel,
        grid=(TOK // part,),
        in_specs=[pl.BlockSpec(memory_space=pltpu.SMEM)]
        + [pl.BlockSpec((CN, part, KV), lambda i: (0, i, 0))] * XN,
        out_specs=pl.BlockSpec((part, WIDTH), lambda i: (i, 0)),
        out_shape=jax.ShapeDtypeStruct((TOK, WIDTH), BF),
        cost_estimate=pl.CostEstimate(flops=0, bytes_accessed=2 << 20, transcendentals=0),
        compiler_params=pltpu.CompilerParams(vmem_limit_bytes=16 << 20),
        name="from_pieces",
    )(jnp.stack(firsts + [x]).astype(jnp.int32), *pieces)


def exchange(array, axes):
    return lax.all_to_all(array, axes, 0, 0, tiled=True)


def spread(array, axes, count):
    return exchange(jnp.broadcast_to(array[None], (count,) + array.shape), axes)


def shifted(array, axes, count, by):
    return lax.ppermute(array, axes, [(i, (i + by) % count) for i in range(count)])


def along_z(array, steps):
    pairs = []
    for z in range(ZH * ZL):
        for core, by in enumerate(steps):
            to = (z + by) % (ZH * ZL)
            pairs.append((((z % ZL) * ZH + z // ZL) * CN + core, ((to % ZL) * ZH + to // ZL) * CN + core))
    return lax.ppermute(array, ("zl", "zh", "core"), pairs)


def hold_kernel(in_ref, *refs):
    refs[-1][...] = in_ref[...]


def hold(array, earlier):
    vmem = pl.BlockSpec(memory_space=pltpu.VMEM)
    return pl.pallas_call(
        hold_kernel,
        in_specs=[vmem] + [pl.BlockSpec(memory_space=pl.ANY)] * len(earlier),
        out_specs=vmem,
        out_shape=jax.ShapeDtypeStruct(array.shape, array.dtype),
        compiler_params=pltpu.CompilerParams(vmem_limit_bytes=16 << 20),
        name="hold",
    )(array, *earlier)


def pair_kernel(core_ref, own_ref, other_ref, out_ref):
    core = core_ref[0]
    out_ref[core] = own_ref[...]
    out_ref[1 - core] = other_ref[...]


def pair(own, other, core):
    vmem = pl.BlockSpec(memory_space=pltpu.VMEM)
    return pl.pallas_call(
        pair_kernel,
        in_specs=[pl.BlockSpec(memory_space=pltpu.SMEM), vmem, vmem],
        out_specs=vmem,
        out_shape=jax.ShapeDtypeStruct((CN,) + own.shape, own.dtype),
        compiler_params=pltpu.CompilerParams(vmem_limit_bytes=16 << 20),
        name="pair",
    )(core[None].astype(jnp.int32), own, other)


def join_kernel(*refs):
    out_ref = refs[-1]
    for i, ref in enumerate(refs[:-2]):
        out_ref[i * 128 : (i + 1) * 128, :] = ref[...]


def join(blocks, earlier):
    vmem = pl.BlockSpec(memory_space=pltpu.VMEM)
    return pl.pallas_call(
        join_kernel,
        in_specs=[vmem] * len(blocks) + [pl.BlockSpec(memory_space=pl.ANY)],
        out_specs=vmem,
        out_shape=jax.ShapeDtypeStruct((len(blocks) * 128, KV), BF),
        compiler_params=pltpu.CompilerParams(vmem_limit_bytes=16 << 20),
        name="join",
    )(*blocks, earlier)


def per_device(inputs, queries, keys, values, out_grad, lengths, value_weight):
    core, x, zl = (lax.axis_index(name) for name in ("core", "x", "zl"))
    with jax.named_scope("cut_inputs"):
        pieces = to_pieces(inputs[0])
    with jax.named_scope("attention"):
        value_grad, key_grad = attend_back(queries[0], keys[0], values[0], out_grad[0], lengths, pieces)
    with jax.named_scope("gather_value_grad"):
        block = hold(value_weight, [value_grad])
        near = [along_z(block, steps) for steps in ((1, -3), (2, -2))]
        mine = hold(lax.all_gather(value_grad, "x", axis=0), near)
        other = shifted(mine, "core", CN, 1)
        grads = pair(mine, other, core).reshape(CN * XN * TOK, KV)
    with jax.named_scope("send_inputs"):
        columns = exchange(pieces, ("core", "x"))
    with jax.named_scope("weight_term"):
        term = lax.dot_general(
            columns.reshape(CN * XN * TOK, KV), grads, (((0,), (0,)), ((), ())), preferred_element_type=F32
        ).astype(BF)
    with jax.named_scope("sum_y"):
        got = exchange(term.reshape(YN, ZL * SUB, KV), "y")
        plane = jnp.sum(got.astype(F32), axis=0).astype(BF).reshape(1, ZL, SUB, KV)
    with jax.named_scope("sum_z"):
        both = jnp.broadcast_to(plane, (ZH, ZL, SUB, KV)).reshape(ZH * ZL, SUB, KV)
        got = exchange(both, ("zh", "zl"))
        total = jnp.sum(got.astype(F32), axis=0) * F32(1.0 / 512)
    with jax.named_scope("share_rows"):
        weight_grad = spread(total.astype(BF), ("core", "y"), QN).reshape(QN * SUB, KV).astype(F32)
    with jax.named_scope("gather_weight"):
        first, last = (along_z(value_weight, steps) for steps in ((0, 4), (3, -1)))
        weight = join([first] + near + [last], plane)
    with jax.named_scope("input_grad"):
        parts = nt(grads, weight).astype(BF).reshape(CN, XN, TOK, KV)
        kept = lax.dynamic_index_in_dim(parts, core, 0, False)
        theirs = shifted(lax.dynamic_index_in_dim(parts, 1 - core, 0, False), "core", CN, 1)
        parts = jnp.stack([kept, theirs], axis=1)
        back = []
        for by in range(XN):
            piece = lax.dynamic_index_in_dim(parts, (x + by) % XN, 0, False)
            back.append(shifted(piece, "x", XN, by) if by else piece)
        input_grad = from_pieces(back, core, zl, x)
    return (input_grad[None], key_grad[None], weight_grad)


def solution(mesh):
    names = ("zl", "x", "y", "zh", "core")
    fine = Mesh(mesh.devices.reshape(ZL, XN, YN, ZH, CN), names)
    blk = names[:2]
    rows = P(names, None, None)
    return jax.shard_map(
        per_device,
        mesh=fine,
        in_specs=(rows, rows, rows, rows, rows, P(names), P(blk, None)),
        out_specs=(rows, rows, P(blk, None)),
        check_vma=False,
    )
```

```python
import jax
import jax.numpy as jnp
from jax import lax
from jax.experimental import pallas as pl
from jax.experimental.pallas import tpu as pltpu
from jax.sharding import Mesh
from jax.sharding import PartitionSpec as P

ZL, XN, YN, ZH, CN = 8, 4, 4, 2, 2
QN = CN * YN
TOK, WIDTH, KV, HD = 128, 4096, 512, 128
GROUP = 8
KV_STEP = 2
SUB = 16
HELD = ZL // CN
BF, F32 = jnp.bfloat16, jnp.float32


def nt(a, b):
    return lax.dot_general(a, b, (((1,), (1,)), ((), ())), preferred_element_type=F32)


def attend_kernel(length_ref, q_ref, k_ref, v_ref, g_ref, _, vg_ref, kg_ref):
    scaling = HD ** (-0.5)
    length = length_ref[0]
    wide = GROUP * TOK
    pos_s = lax.broadcasted_iota(jnp.int32, (TOK, wide), 0)
    pos_t = lax.broadcasted_iota(jnp.int32, (TOK, wide), 1) & (TOK - 1)
    allowed = pos_s <= pos_t
    live = ((lax.broadcasted_iota(jnp.int32, (1, wide), 1) & (TOK - 1)) < length).astype(F32)
    for head in range(KV_STEP):
        cols = slice(head * HD, (head + 1) * HD)
        heads = range(head * GROUP, (head + 1) * GROUP)
        qs = jnp.concatenate([q_ref[:, h * HD : (h + 1) * HD] for h in heads], axis=0)
        gs = jnp.concatenate([g_ref[:, h * HD : (h + 1) * HD] for h in heads], axis=0)
        scores = jnp.where(allowed, nt(k_ref[:, cols], qs) * scaling, F32(-1e30))
        expd = jnp.exp(scores - jnp.max(scores, axis=0, keepdims=True))
        probs = expd * (live / jnp.sum(expd, axis=0, keepdims=True))
        dprob = nt(v_ref[:, cols], gs)
        delta = jnp.sum(probs * dprob, axis=0, keepdims=True)
        dscore = probs * (dprob - delta)
        vg = jnp.dot(probs.astype(BF), gs, preferred_element_type=F32)
        kg = jnp.dot(dscore.astype(BF), qs, preferred_element_type=F32)
        vg_ref[:, cols] = vg.astype(BF)
        kg_ref[:, cols] = (kg * scaling).astype(BF)


def attend_back(query, key_rows, value_rows, grad_rows, length, earlier):
    wide = pl.BlockSpec((TOK, KV_STEP * GROUP * HD), lambda g: (0, g))
    thin = pl.BlockSpec((TOK, KV_STEP * HD), lambda g: (0, g))
    return pl.pallas_call(
        attend_kernel,
        grid=(KV // HD // KV_STEP,),
        in_specs=[pl.BlockSpec(memory_space=pltpu.SMEM), wide, thin, thin, wide, pl.BlockSpec(memory_space=pl.ANY)],
        out_specs=[thin, thin],
        out_shape=[jax.ShapeDtypeStruct((TOK, KV), BF)] * 2,
        cost_estimate=pl.CostEstimate(
            flops=10 * 32 * TOK * TOK * HD, bytes_accessed=3 << 20, transcendentals=32 * TOK * TOK
        ),
        name="attend",
    )(length, query, key_rows, value_rows, grad_rows, earlier)


def swap_groups(tiles):
    lane = lax.broadcasted_iota(jnp.int32, tiles[0].shape, 1)
    for bit in (1, 2, 4):
        shift = bit * SUB
        high = (lane & shift) != 0
        after = list(tiles)
        for i in range(8):
            if i & bit == 0:
                low_tile, high_tile = tiles[i], tiles[i | bit]
                after[i] = jnp.where(high, pltpu.roll(high_tile, shift, 1), low_tile)
                after[i | bit] = jnp.where(high, high_tile, pltpu.roll(low_tile, 128 - shift, 1))
        tiles = after
    return tiles


def to_pieces_kernel(in_ref, out_ref):
    for x in range(XN):
        tiles = [in_ref[:, (zl * XN + x) * 128 : (zl * XN + x + 1) * 128].astype(F32) for zl in range(8)]
        for q, tile in enumerate(swap_groups(tiles)):
            y = q % YN
            out_ref[q // YN * XN + x, :, y * 128 : (y + 1) * 128] = tile.astype(BF)


def from_pieces_kernel(at_ref, *refs):
    out_ref = refs[-1]
    for by in range(XN):
        x = (at_ref[2] + XN - by) % XN
        for which in range(CN):
            for k in range(HELD):
                tile = (at_ref[which] + ZL - k) % ZL * XN + x
                lanes = pl.ds(pl.multiple_of(tile * 128, 128), 128)
                out_ref[:, lanes] = refs[by][which, :, k * 128 : (k + 1) * 128]


def to_pieces(rows):
    part = 64
    return pl.pallas_call(
        to_pieces_kernel,
        grid=(TOK // part,),
        in_specs=[pl.BlockSpec((part, WIDTH), lambda i: (i, 0))],
        out_specs=pl.BlockSpec((QN, part, KV), lambda i: (0, i, 0)),
        out_shape=jax.ShapeDtypeStruct((QN, TOK, KV), BF),
        cost_estimate=pl.CostEstimate(flops=1 << 22, bytes_accessed=2 << 20, transcendentals=0),
        name="to_pieces",
    )(rows)


def from_pieces(pieces, core, zl, x):
    part = 64
    firsts = [(zl + ZL - HELD * c) % ZL for c in (core, 1 - core)]
    return pl.pallas_call(
        from_pieces_kernel,
        grid=(TOK // part,),
        in_specs=[pl.BlockSpec(memory_space=pltpu.SMEM)]
        + [pl.BlockSpec((CN, part, KV), lambda i: (0, i, 0))] * XN,
        out_specs=pl.BlockSpec((part, WIDTH), lambda i: (i, 0)),
        out_shape=jax.ShapeDtypeStruct((TOK, WIDTH), BF),
        cost_estimate=pl.CostEstimate(flops=0, bytes_accessed=2 << 20, transcendentals=0),
        compiler_params=pltpu.CompilerParams(vmem_limit_bytes=16 << 20),
        name="from_pieces",
    )(jnp.stack(firsts + [x]).astype(jnp.int32), *pieces)


def exchange(array, axes):
    return lax.all_to_all(array, axes, 0, 0, tiled=True)


def spread(array, axes, count):
    return exchange(jnp.broadcast_to(array[None], (count,) + array.shape), axes)


def shifted(array, axes, count, by):
    return lax.ppermute(array, axes, [(i, (i + by) % count) for i in range(count)])


def along_z(array, steps):
    pairs = []
    for z in range(ZH * ZL):
        for core, by in enumerate(steps):
            to = (z + by) % (ZH * ZL)
            pairs.append((((z % ZL) * ZH + z // ZL) * CN + core, ((to % ZL) * ZH + to // ZL) * CN + core))
    return lax.ppermute(array, ("zl", "zh", "core"), pairs)


def hold_kernel(in_ref, *refs):
    refs[-1][...] = in_ref[...]


def hold(array, earlier):
    vmem = pl.BlockSpec(memory_space=pltpu.VMEM)
    return pl.pallas_call(
        hold_kernel,
        in_specs=[vmem] + [pl.BlockSpec(memory_space=pl.ANY)] * len(earlier),
        out_specs=vmem,
        out_shape=jax.ShapeDtypeStruct(array.shape, array.dtype),
        compiler_params=pltpu.CompilerParams(vmem_limit_bytes=16 << 20),
        name="hold",
    )(array, *earlier)


def pair_kernel(core_ref, own_ref, other_ref, out_ref):
    core = core_ref[0]
    out_ref[core] = own_ref[...]
    out_ref[1 - core] = other_ref[...]


def pair(own, other, core):
    vmem = pl.BlockSpec(memory_space=pltpu.VMEM)
    return pl.pallas_call(
        pair_kernel,
        in_specs=[pl.BlockSpec(memory_space=pltpu.SMEM), vmem, vmem],
        out_specs=vmem,
        out_shape=jax.ShapeDtypeStruct((CN,) + own.shape, own.dtype),
        compiler_params=pltpu.CompilerParams(vmem_limit_bytes=16 << 20),
        name="pair",
    )(core[None].astype(jnp.int32), own, other)


def join_kernel(*refs):
    out_ref = refs[-1]
    for i, ref in enumerate(refs[:-2]):
        out_ref[i * 128 : (i + 1) * 128, :] = ref[...]


def join(blocks, earlier):
    vmem = pl.BlockSpec(memory_space=pltpu.VMEM)
    return pl.pallas_call(
        join_kernel,
        in_specs=[vmem] * len(blocks) + [pl.BlockSpec(memory_space=pl.ANY)],
        out_specs=vmem,
        out_shape=jax.ShapeDtypeStruct((len(blocks) * 128, KV), BF),
        compiler_params=pltpu.CompilerParams(vmem_limit_bytes=16 << 20),
        name="join",
    )(*blocks, earlier)


def per_device(inputs, queries, keys, values, out_grad, lengths, value_weight):
    core, x, zl = (lax.axis_index(name) for name in ("core", "x", "zl"))
    with jax.named_scope("cut_inputs"):
        pieces = to_pieces(inputs[0])
    with jax.named_scope("attention"):
        value_grad, key_grad = attend_back(queries[0], keys[0], values[0], out_grad[0], lengths, pieces)
    with jax.named_scope("gather_value_grad"):
        early = along_z(value_weight, (2, -2))
        mine = hold(lax.all_gather(value_grad, "x", axis=0), [early])
        other = shifted(mine, "core", CN, 1)
        grads = pair(mine, other, core).reshape(CN * XN * TOK, KV)
    with jax.named_scope("send_inputs"):
        columns = exchange(pieces, ("core", "x"))
    with jax.named_scope("weight_term"):
        term = lax.dot_general(
            columns.reshape(CN * XN * TOK, KV), grads, (((0,), (0,)), ((), ())), preferred_element_type=F32
        ).astype(BF)
    with jax.named_scope("sum_y"):
        got = exchange(term.reshape(YN, ZL * SUB, KV), "y")
        plane = jnp.sum(got.astype(F32), axis=0).astype(BF).reshape(1, ZL, SUB, KV)
    with jax.named_scope("sum_z"):
        both = jnp.broadcast_to(plane, (ZH, ZL, SUB, KV)).reshape(ZH * ZL, SUB, KV)
        got = exchange(both, ("zh", "zl"))
        total = jnp.sum(got.astype(F32), axis=0) * F32(1.0 / 512)
    with jax.named_scope("share_rows"):
        weight_grad = spread(total.astype(BF), ("core", "y"), QN).reshape(QN * SUB, KV).astype(F32)
    with jax.named_scope("gather_weight"):
        first, second, last = (along_z(value_weight, steps) for steps in ((0, 4), (1, -3), (3, -1)))
        weight = join([first, second, early, last], plane)
    with jax.named_scope("input_grad"):
        parts = nt(grads, weight).astype(BF).reshape(CN, XN, TOK, KV)
        kept = lax.dynamic_index_in_dim(parts, core, 0, False)
        theirs = shifted(lax.dynamic_index_in_dim(parts, 1 - core, 0, False), "core", CN, 1)
        parts = jnp.stack([kept, theirs], axis=1)
        back = []
        for by in range(XN):
            piece = lax.dynamic_index_in_dim(parts, (x + by) % XN, 0, False)
            back.append(shifted(piece, "x", XN, by) if by else piece)
        input_grad = from_pieces(back, core, zl, x)
    return (input_grad[None], key_grad[None], weight_grad)


def solution(mesh):
    names = ("zl", "x", "y", "zh", "core")
    fine = Mesh(mesh.devices.reshape(ZL, XN, YN, ZH, CN), names)
    blk = names[:2]
    rows = P(names, None, None)
    return jax.shard_map(
        per_device,
        mesh=fine,
        in_specs=(rows, rows, rows, rows, rows, P(names), P(blk, None)),
        out_specs=(rows, rows, P(blk, None)),
        check_vma=False,
    )
```

```python
import jax
import jax.numpy as jnp
from jax import lax
from jax.experimental import pallas as pl
from jax.experimental.pallas import tpu as pltpu
from jax.sharding import Mesh
from jax.sharding import PartitionSpec as P

ZL, XN, YN, ZH, CN = 8, 4, 4, 2, 2
QN = CN * YN
TOK, WIDTH, KV, HD = 128, 4096, 512, 128
GROUP = 8
KV_STEP = 2
SUB = 16
HELD = ZL // CN
BF, F32 = jnp.bfloat16, jnp.float32


def nt(a, b):
    return lax.dot_general(a, b, (((1,), (1,)), ((), ())), preferred_element_type=F32)


def attend_kernel(length_ref, q_ref, k_ref, v_ref, g_ref, _, vg_ref, kg_ref):
    scaling = HD ** (-0.5)
    length = length_ref[0]
    wide = GROUP * TOK
    pos_s = lax.broadcasted_iota(jnp.int32, (TOK, wide), 0)
    pos_t = lax.broadcasted_iota(jnp.int32, (TOK, wide), 1) & (TOK - 1)
    allowed = pos_s <= pos_t
    live = ((lax.broadcasted_iota(jnp.int32, (1, wide), 1) & (TOK - 1)) < length).astype(F32)
    for head in range(KV_STEP):
        cols = slice(head * HD, (head + 1) * HD)
        heads = range(head * GROUP, (head + 1) * GROUP)
        qs = jnp.concatenate([q_ref[:, h * HD : (h + 1) * HD] for h in heads], axis=0)
        gs = jnp.concatenate([g_ref[:, h * HD : (h + 1) * HD] for h in heads], axis=0)
        scores = jnp.where(allowed, nt(k_ref[:, cols], qs) * scaling, F32(-1e30))
        expd = jnp.exp(scores - jnp.max(scores, axis=0, keepdims=True))
        probs = expd * (live / jnp.sum(expd, axis=0, keepdims=True))
        dprob = nt(v_ref[:, cols], gs)
        delta = jnp.sum(probs * dprob, axis=0, keepdims=True)
        dscore = probs * (dprob - delta)
        vg = jnp.dot(probs.astype(BF), gs, preferred_element_type=F32)
        kg = jnp.dot(dscore.astype(BF), qs, preferred_element_type=F32)
        vg_ref[:, cols] = vg.astype(BF)
        kg_ref[:, cols] = (kg * scaling).astype(BF)


def attend_back(query, key_rows, value_rows, grad_rows, length, earlier):
    wide = pl.BlockSpec((TOK, KV_STEP * GROUP * HD), lambda g: (0, g))
    thin = pl.BlockSpec((TOK, KV_STEP * HD), lambda g: (0, g))
    return pl.pallas_call(
        attend_kernel,
        grid=(KV // HD // KV_STEP,),
        in_specs=[pl.BlockSpec(memory_space=pltpu.SMEM), wide, thin, thin, wide, pl.BlockSpec(memory_space=pl.ANY)],
        out_specs=[thin, thin],
        out_shape=[jax.ShapeDtypeStruct((TOK, KV), BF)] * 2,
        cost_estimate=pl.CostEstimate(
            flops=10 * 32 * TOK * TOK * HD, bytes_accessed=3 << 20, transcendentals=32 * TOK * TOK
        ),
        name="attend",
    )(length, query, key_rows, value_rows, grad_rows, earlier)


def swap_groups(tiles):
    lane = lax.broadcasted_iota(jnp.int32, tiles[0].shape, 1)
    for bit in (1, 2, 4):
        shift = bit * SUB
        high = (lane & shift) != 0
        after = list(tiles)
        for i in range(8):
            if i & bit == 0:
                low_tile, high_tile = tiles[i], tiles[i | bit]
                after[i] = jnp.where(high, pltpu.roll(high_tile, shift, 1), low_tile)
                after[i | bit] = jnp.where(high, high_tile, pltpu.roll(low_tile, 128 - shift, 1))
        tiles = after
    return tiles


def to_pieces_kernel(in_ref, out_ref):
    for x in range(XN):
        tiles = [in_ref[:, (zl * XN + x) * 128 : (zl * XN + x + 1) * 128].astype(F32) for zl in range(8)]
        for q, tile in enumerate(swap_groups(tiles)):
            y = q % YN
            out_ref[q // YN * XN + x, :, y * 128 : (y + 1) * 128] = tile.astype(BF)


def from_pieces_kernel(at_ref, *refs):
    out_ref = refs[-1]
    for by in range(XN):
        x = (at_ref[2] + XN - by) % XN
        for which in range(CN):
            for k in range(HELD):
                tile = (at_ref[which] + ZL - k) % ZL * XN + x
                lanes = pl.ds(pl.multiple_of(tile * 128, 128), 128)
                out_ref[:, lanes] = refs[by][which, :, k * 128 : (k + 1) * 128]


def to_pieces(rows):
    part = 64
    return pl.pallas_call(
        to_pieces_kernel,
        grid=(TOK // part,),
        in_specs=[pl.BlockSpec((part, WIDTH), lambda i: (i, 0))],
        out_specs=pl.BlockSpec((QN, part, KV), lambda i: (0, i, 0)),
        out_shape=jax.ShapeDtypeStruct((QN, TOK, KV), BF),
        cost_estimate=pl.CostEstimate(flops=1 << 22, bytes_accessed=2 << 20, transcendentals=0),
        name="to_pieces",
    )(rows)


def from_pieces(pieces, core, zl, x):
    part = 64
    firsts = [(zl + ZL - HELD * c) % ZL for c in (core, 1 - core)]
    return pl.pallas_call(
        from_pieces_kernel,
        grid=(TOK // part,),
        in_specs=[pl.BlockSpec(memory_space=pltpu.SMEM)]
        + [pl.BlockSpec((CN, part, KV), lambda i: (0, i, 0))] * XN,
        out_specs=pl.BlockSpec((part, WIDTH), lambda i: (i, 0)),
        out_shape=jax.ShapeDtypeStruct((TOK, WIDTH), BF),
        cost_estimate=pl.CostEstimate(flops=0, bytes_accessed=2 << 20, transcendentals=0),
        compiler_params=pltpu.CompilerParams(vmem_limit_bytes=16 << 20),
        name="from_pieces",
    )(jnp.stack(firsts + [x]).astype(jnp.int32), *pieces)


def exchange(array, axes):
    return lax.all_to_all(array, axes, 0, 0, tiled=True)


def spread(array, axes, count):
    return exchange(jnp.broadcast_to(array[None], (count,) + array.shape), axes)


def shifted(array, axes, count, by):
    return lax.ppermute(array, axes, [(i, (i + by) % count) for i in range(count)])


def along_z(array, steps):
    pairs = []
    for z in range(ZH * ZL):
        for core, by in enumerate(steps):
            to = (z + by) % (ZH * ZL)
            pairs.append((((z % ZL) * ZH + z // ZL) * CN + core, ((to % ZL) * ZH + to // ZL) * CN + core))
    return lax.ppermute(array, ("zl", "zh", "core"), pairs)


def hold_kernel(in_ref, *refs):
    refs[-1][...] = in_ref[...]


def hold(array, earlier):
    vmem = pl.BlockSpec(memory_space=pltpu.VMEM)
    return pl.pallas_call(
        hold_kernel,
        in_specs=[vmem] + [pl.BlockSpec(memory_space=pl.ANY)] * len(earlier),
        out_specs=vmem,
        out_shape=jax.ShapeDtypeStruct(array.shape, array.dtype),
        compiler_params=pltpu.CompilerParams(vmem_limit_bytes=16 << 20),
        name="hold",
    )(array, *earlier)


def pair_kernel(core_ref, own_ref, other_ref, out_ref):
    core = core_ref[0]
    out_ref[core] = own_ref[...]
    out_ref[1 - core] = other_ref[...]


def pair(own, other, core):
    vmem = pl.BlockSpec(memory_space=pltpu.VMEM)
    return pl.pallas_call(
        pair_kernel,
        in_specs=[pl.BlockSpec(memory_space=pltpu.SMEM), vmem, vmem],
        out_specs=vmem,
        out_shape=jax.ShapeDtypeStruct((CN,) + own.shape, own.dtype),
        compiler_params=pltpu.CompilerParams(vmem_limit_bytes=16 << 20),
        name="pair",
    )(core[None].astype(jnp.int32), own, other)


def join_kernel(*refs):
    out_ref = refs[-1]
    for i, ref in enumerate(refs[:-2]):
        out_ref[i * 128 : (i + 1) * 128, :] = ref[...]


def join(blocks, earlier):
    vmem = pl.BlockSpec(memory_space=pltpu.VMEM)
    return pl.pallas_call(
        join_kernel,
        in_specs=[vmem] * len(blocks) + [pl.BlockSpec(memory_space=pl.ANY)],
        out_specs=vmem,
        out_shape=jax.ShapeDtypeStruct((len(blocks) * 128, KV), BF),
        compiler_params=pltpu.CompilerParams(vmem_limit_bytes=16 << 20),
        name="join",
    )(*blocks, earlier)


def per_device(inputs, queries, keys, values, out_grad, lengths, value_weight):
    core, x, zl = (lax.axis_index(name) for name in ("core", "x", "zl"))
    with jax.named_scope("cut_inputs"):
        pieces = to_pieces(inputs[0])
    with jax.named_scope("attention"):
        value_grad, key_grad = attend_back(queries[0], keys[0], values[0], out_grad[0], lengths, pieces)
    with jax.named_scope("gather_value_grad"):
        early = along_z(value_weight, (0, 4))
        mine = hold(lax.all_gather(value_grad, "x", axis=0), [early])
        other = shifted(mine, "core", CN, 1)
        grads = pair(mine, other, core).reshape(CN * XN * TOK, KV)
    with jax.named_scope("send_inputs"):
        columns = exchange(pieces, ("core", "x"))
    with jax.named_scope("weight_term"):
        term = lax.dot_general(
            columns.reshape(CN * XN * TOK, KV), grads, (((0,), (0,)), ((), ())), preferred_element_type=F32
        ).astype(BF)
    with jax.named_scope("sum_y"):
        got = exchange(term.reshape(YN, ZL * SUB, KV), "y")
        plane = jnp.sum(got.astype(F32), axis=0).astype(BF).reshape(1, ZL, SUB, KV)
    with jax.named_scope("sum_z"):
        both = jnp.broadcast_to(plane, (ZH, ZL, SUB, KV)).reshape(ZH * ZL, SUB, KV)
        got = exchange(both, ("zh", "zl"))
        total = jnp.sum(got.astype(F32), axis=0) * F32(1.0 / 512)
    with jax.named_scope("share_rows"):
        weight_grad = spread(total.astype(BF), ("core", "y"), QN).reshape(QN * SUB, KV).astype(F32)
    with jax.named_scope("gather_weight"):
        later = [along_z(value_weight, steps) for steps in ((1, -3), (2, -2), (3, -1))]
        weight = join([early] + later, plane)
    with jax.named_scope("input_grad"):
        parts = nt(grads, weight).astype(BF).reshape(CN, XN, TOK, KV)
        kept = lax.dynamic_index_in_dim(parts, core, 0, False)
        theirs = shifted(lax.dynamic_index_in_dim(parts, 1 - core, 0, False), "core", CN, 1)
        parts = jnp.stack([kept, theirs], axis=1)
        back = []
        for by in range(XN):
            piece = lax.dynamic_index_in_dim(parts, (x + by) % XN, 0, False)
            back.append(shifted(piece, "x", XN, by) if by else piece)
        input_grad = from_pieces(back, core, zl, x)
    return (input_grad[None], key_grad[None], weight_grad)


def solution(mesh):
    names = ("zl", "x", "y", "zh", "core")
    fine = Mesh(mesh.devices.reshape(ZL, XN, YN, ZH, CN), names)
    blk = names[:2]
    rows = P(names, None, None)
    return jax.shard_map(
        per_device,
        mesh=fine,
        in_specs=(rows, rows, rows, rows, rows, P(names), P(blk, None)),
        out_specs=(rows, rows, P(blk, None)),
        check_vma=False,
    )
```
